512 devices in a mesh: lat: 16 (over x_lo, y), lon: 32 (over x_hi, z, core).
Axes of the slice: x: 4 (x_hi: 2, x_lo: 2; x = x_hi * 2 + x_lo), y: 8, z: 8, core: 2. Of those that a mesh axis runs over, the one named last changes fastest.
Arguments:
- tokens: bfloat16 [2, 192, 768, 192], P(None, 'lat', 'lon'), may hold values from -6 to 6
- norm_gain: float32 [192], replicated, may hold values from 0.1 to 1.9
- qkv_weight: bfloat16 [192, 576], replicated, may hold values from -0.4375 to 0.4375
- proj_weight: bfloat16 [192, 192], replicated, may hold values from -0.4375 to 0.4375
- merge_gain: float32 [768], replicated, may hold values from 0.1 to 1.9
- merge_weight: bfloat16 [768, 384], replicated, may hold values from -0.21875 to 0.21875
- coarse_gain: float32 [384], replicated, may hold values from 0.1 to 1.9
- coarse_qkv: bfloat16 [384, 1152], replicated, may hold values from -0.3125 to 0.3125
- coarse_proj: bfloat16 [384, 384], replicated, may hold values from -0.3125 to 0.3125
- up_weight: bfloat16 [384, 768], replicated, may hold values from -0.3125 to 0.3125
- up_gain: float32 [192], replicated, may hold values from 0.1 to 1.9
- out_weight: bfloat16 [192, 192], replicated, may hold values from -0.4375 to 0.4375
Outputs:
- encoded: bfloat16 [2, 192, 768, 192], P(None, 'lat', 'lon')
The draws below stay inside these ranges and needn't reach their ends.
All inputs are finite; a program needn't handle non-finite values.
Results may differ from the reference program's by a relative error of at most 0.02.
Values may be sent and summed in bfloat16 or wider, within the bound.
A program may use at most 64 MiB of HBM per device.

```python
import jax
import jax.numpy as jnp
from jax import lax

WIDTH = 192
COARSE_WIDTH = 384
FINE_HEADS = 6
COARSE_HEADS = 12
LEVELS = 2
WIN_LAT = 6
WIN_LON = 12
NLAT = 192
NLON = 768


def block_scale(rng, dims, shards, least, high):
    loudness, own = 1.0, jax.random.fold_in(rng, 6)
    for position, blocks in shards:
        heights = jnp.exp(jax.random.uniform(jax.random.fold_in(own, position), (blocks,), jnp.float32, least / len(shards), high / len(shards)))
        loudness = loudness * jnp.repeat(heights, dims[position] // blocks).reshape([-1 if axis == position else 1 for axis in range(len(dims))])
    return loudness


def noise(stream_key, extent, width, bound, split=(), kind=jnp.bfloat16):
    level = block_scale(stream_key, extent, split, -0.22, 0.18) if split else 1.0
    entries = jax.random.normal(stream_key, extent, jnp.float32) * width * level
    return jnp.minimum(jnp.maximum(entries, -bound), bound).astype(kind)


def setup_inputs(seed: int = 0) -> dict:
    splits = jax.random.split(jax.random.key(seed), 13)
    tokens = noise(splits[0], (LEVELS, NLAT, NLON, WIDTH), 1.0, 6.0, ((1, 16), (2, 32)))
    norm_gain = jnp.clip(1.0 + 0.18 * jax.random.normal(splits[1], (WIDTH,), jnp.float32), 0.1, 1.9)
    qkv_weight = noise(splits[2], (WIDTH, 3 * WIDTH), WIDTH ** -0.5, 0.4375)
    proj_weight = noise(splits[3], (WIDTH, WIDTH), WIDTH ** -0.5, 0.4375)
    merge_gain = jnp.clip(1.0 + 0.18 * jax.random.normal(splits[4], (4 * WIDTH,), jnp.float32), 0.1, 1.9)
    merge_weight = noise(splits[5], (4 * WIDTH, COARSE_WIDTH), (4 * WIDTH) ** -0.5, 0.21875)
    coarse_gain = jnp.clip(1.0 + 0.18 * jax.random.normal(splits[6], (COARSE_WIDTH,), jnp.float32), 0.1, 1.9)
    coarse_qkv = noise(splits[7], (COARSE_WIDTH, 3 * COARSE_WIDTH), COARSE_WIDTH ** -0.5, 0.3125)
    coarse_proj = noise(splits[8], (COARSE_WIDTH, COARSE_WIDTH), COARSE_WIDTH ** -0.5, 0.3125)
    up_weight = noise(splits[9], (COARSE_WIDTH, 4 * WIDTH), COARSE_WIDTH ** -0.5, 0.3125)
    up_gain = jnp.clip(1.0 + 0.18 * jax.random.normal(splits[10], (WIDTH,), jnp.float32), 0.1, 1.9)
    out_weight = noise(splits[11], (WIDTH, WIDTH), WIDTH ** -0.5, 0.4375)
    return {"tokens": tokens, "norm_gain": norm_gain, "qkv_weight": qkv_weight, "proj_weight": proj_weight, "merge_gain": merge_gain, "merge_weight": merge_weight, "coarse_gain": coarse_gain, "coarse_qkv": coarse_qkv, "coarse_proj": coarse_proj, "up_weight": up_weight, "up_gain": up_gain, "out_weight": out_weight}


EPSILON = 1e-05

def layer_norm(values, norm_gain):
    average = lax.optimization_barrier(jnp.mean(values, axis=-1, keepdims=True))
    centred = values - average
    spread = lax.optimization_barrier(jnp.mean(centred * centred, axis=-1, keepdims=True))
    return (centred * lax.rsqrt(spread + EPSILON) * norm_gain).astype(jnp.bfloat16)

def window_heads(stripe, norm_gain, qkv_weight, head_count, lat_pair):
    levels, row_count, col_count, channels = stripe.shape
    head_dim = channels // head_count
    normed = layer_norm(stripe.astype(jnp.float32), norm_gain.astype(jnp.float32))
    packed = jnp.dot(normed.reshape(-1, channels), qkv_weight, preferred_element_type=jnp.float32).astype(jnp.bfloat16)
    packed = packed.reshape(levels // 2, 2, row_count, col_count // WIN_LON, WIN_LON, 3, head_count, head_dim)
    packed = packed.transpose(0, 3, 5, 6, 1, 2, 4, 7)
    window_len = 2 * row_count * WIN_LON
    packed = packed.reshape(levels // 2, col_count // WIN_LON, 3, head_count, window_len, head_dim)
    queries = packed[:, :, 0].astype(jnp.float32)
    key_block = packed[:, :, 1].astype(jnp.float32)
    value_block = packed[:, :, 2].astype(jnp.float32)
    scores = jnp.einsum('abhtd,abhsd->abhts', queries, key_block) * head_dim ** (-0.5)
    level_ids = jnp.arange(levels // 2)
    diagonal = jnp.eye(2, dtype=jnp.bool_)
    level_mask = (level_ids[:, None, None] != levels // 2 - 1) | diagonal[None]
    allowed = level_mask[:, :, None, None, :, None, None] & lat_pair[None, None, :, None, None, :, None]
    allowed = jnp.broadcast_to(allowed, (levels // 2, 2, row_count, WIN_LON, 2, row_count, WIN_LON))
    allowed = allowed.reshape(levels // 2, window_len, window_len)
    raised = jnp.where(allowed[:, None, None], jnp.exp(scores), 0.0)
    weights = (raised / lax.optimization_barrier(jnp.sum(raised, axis=-1, keepdims=True))).astype(jnp.bfloat16)
    attended = jnp.einsum('abhts,abhsd->abhtd', weights.astype(jnp.float32), value_block).astype(jnp.bfloat16)
    attended = attended.reshape(levels // 2, col_count // WIN_LON, head_count, 2, row_count, WIN_LON, head_dim)
    attended = attended.transpose(0, 3, 4, 1, 5, 2, 6).reshape(levels, row_count, col_count, channels)
    return attended

def shifted_block(grid_in, norm_gain, qkv_weight, proj_weight, head_count):
    levels, lat_count, lon_count, channels = grid_in.shape
    half_lat = WIN_LAT // 2
    half_lon = WIN_LON // 2
    rolled = jnp.roll(grid_in, (-1, -half_lat, -half_lon), axis=(0, 1, 2))
    strips = lat_count // WIN_LAT
    grouped = rolled.reshape(levels, strips, WIN_LAT, lon_count, channels).transpose(1, 0, 2, 3, 4)
    upper_half = jnp.arange(WIN_LAT) < half_lat
    split_pairs = upper_half[:, None] == upper_half[None, :]

    def one_strip(packet):
        stripe, strip_index = packet
        lat_pair = split_pairs | (strip_index != strips - 1)
        attended = window_heads(stripe, norm_gain, qkv_weight, head_count, lat_pair)
        branch = jnp.dot(attended.reshape(-1, channels), proj_weight, preferred_element_type=jnp.float32)
        return (stripe.astype(jnp.float32) + branch.reshape(stripe.shape)).astype(jnp.bfloat16)
    summed = lax.map(one_strip, (grouped, jnp.arange(strips, dtype=jnp.int32)))
    summed = summed.transpose(1, 0, 2, 3, 4).reshape(levels, lat_count, lon_count, channels)
    return jnp.roll(summed, (1, half_lat, half_lon), axis=(0, 1, 2))

def merge_patches(fine_out, merge_gain, merge_weight):
    levels, lat_count, lon_count, channels = fine_out.shape
    stacked = fine_out.reshape(levels, lat_count // 2, 2, lon_count // 2, 2, channels)
    stacked = stacked.transpose(0, 1, 3, 4, 2, 5).reshape(levels, lat_count // 2, lon_count // 2, 4 * channels)
    normed = layer_norm(stacked.astype(jnp.float32), merge_gain.astype(jnp.float32))
    merged = jnp.dot(normed.reshape(-1, 4 * channels), merge_weight, preferred_element_type=jnp.float32)
    return merged.astype(jnp.bfloat16).reshape(levels, lat_count // 2, lon_count // 2, merge_weight.shape[1])

def expand(coarse_out, fine_out, up_weight, up_gain, out_weight):
    levels, lat_count, lon_count, coarse_width = coarse_out.shape
    channels = fine_out.shape[-1]
    lifted = jnp.dot(coarse_out.reshape(-1, coarse_width), up_weight, preferred_element_type=jnp.float32)
    lifted = lifted.reshape(levels, lat_count, lon_count, 2, 2, channels)
    lifted = lifted.transpose(0, 1, 4, 2, 3, 5).reshape(levels, 2 * lat_count, 2 * lon_count, channels)
    normed = layer_norm(lifted, up_gain.astype(jnp.float32))
    branch = jnp.dot(normed.reshape(-1, channels), out_weight, preferred_element_type=jnp.float32)
    return (fine_out.astype(jnp.float32) + branch.reshape(fine_out.shape)).astype(jnp.bfloat16)

def reference(tokens, norm_gain, qkv_weight, proj_weight, merge_gain, merge_weight, coarse_gain, coarse_qkv, coarse_proj, up_weight, up_gain, out_weight):
    fine_out = shifted_block(tokens, norm_gain, qkv_weight, proj_weight, FINE_HEADS)
    coarse = merge_patches(fine_out, merge_gain, merge_weight)
    coarse_out = shifted_block(coarse, coarse_gain, coarse_qkv, coarse_proj, COARSE_HEADS)
    return expand(coarse_out, fine_out, up_weight, up_gain, out_weight)
```

```python
import functools

import jax
import jax.numpy as jnp
import ml_dtypes
import numpy as np
from jax import lax
from jax.experimental import pallas as pl
from jax.experimental.pallas import tpu as pltpu
from jax.sharding import PartitionSpec as P

MESH = pl.DeviceIdType.MESH
BF = jnp.bfloat16
F32 = jnp.float32
EPSILON = 1e-05
C = 192
CC = 384
ROWS, COLS = 12, 24
OWN = ROWS * COLS
UNIT = 18
WIN = 72
PAD = 80
HEAD = 32
Q_SCALE = float(HEAD**-0.5 * np.log2(np.e))
V_SCALE = 2.0**-8
FAR = -1e30
HALO = 160
LAT_AT, LON_AT, DIAG_AT = 0, 64, 128


def one_hot(rows, cols, pairs):
    out = np.zeros((rows, cols), np.float32)
    for r, c in pairs:
        out[r, c] = 1.0
    return out.astype(ml_dtypes.bfloat16)


def halo_slot(unit_of):
    for j in range(3):
        yield LAT_AT + j * UNIT, (0, j + 1)
        yield LON_AT + j * UNIT, (j + 1, 0)
    yield DIAG_AT, (0, 0)


def received(a, b):
    if a == 3 and b == 3:
        return DIAG_AT
    if a == 3:
        return LAT_AT + b * UNIT
    if b == 3:
        return LON_AT + a * UNIT
    return None


def window_row(a, b):
    return ((a // 2) * 2 + b // 2) * PAD + ((a % 2) * 2 + b % 2) * UNIT


def natural(level, r, c):
    n = r * COLS + c
    return n if level == 0 else OWN - 1 - n


@functools.cache
def tables():
    units = [(a, b) for a in range(4) for b in range(4)]
    send1, gather1, final = [], [], []
    for level in range(2):

        def own(a, b, t, level=level):
            return natural(level, a * 3 + t // 6, b * 6 + t % 6)

        send1.append(
            one_hot(HALO, OWN, [(s + t, own(a, b, t)) for s, (a, b) in halo_slot(None) for t in range(UNIT)])
        )
        pairs = []
        for a, b in units:
            slot = received(a, b)
            for t in range(UNIT):
                source = own(a + 1, b + 1, t) if slot is None else OWN + slot + t
                pairs.append((window_row(a, b) + t, source))
        gather1.append(one_hot(4 * PAD, OWN + HALO, pairs))
        pairs = []
        for r in range(ROWS):
            for c in range(COLS):
                qr, qc = int(r < 6), int(c < 12)
                y, x = r % 6, c % 12
                k = y % 2 + 2 * (x % 2)
                t = (y // 2) * 6 + x // 2
                pairs.append((natural(level, r, c), (qr * 2 + qc) * PAD + k * UNIT + t))
        final.append(one_hot(OWN, 4 * PAD, pairs))
    send2 = one_hot(
        HALO, 4 * PAD, [(s + t, window_row(a, b) + t) for s, (a, b) in halo_slot(None) for t in range(UNIT)]
    )
    pairs = []
    for y in range(ROWS):
        for x in range(COLS):
            a, b, t = y // 3, x // 6, (y % 3) * 6 + x % 6
            slot = received(a, b)
            source = window_row(a + 1, b + 1) + t if slot is None else 4 * PAD + slot + t
            k = y % 2 + 2 * (x % 2)
            i, j = y // 2, x // 2
            cell = ((i // 3) * 2 + j // 6) * UNIT + (i % 3) * 6 + j % 6
            pairs.append((k * PAD + cell, source))
    gather2 = one_hot(4 * PAD, 4 * PAD + HALO, pairs)
    pairs = []
    for quarter in range(4):
        for k in range(4):
            for t in range(UNIT):
                pairs.append((quarter * PAD + k * UNIT + t, k * PAD + quarter * UNIT + t))
    send3 = one_hot(4 * PAD, 4 * PAD, pairs)
    ones4 = np.zeros((4 * PAD, 128), np.float32)
    ones2 = np.zeros((2 * PAD, 128), np.float32)
    for h in range(4):
        ones4[h * PAD : h * PAD + WIN, h * HEAD : (h + 1) * HEAD] = 1.0
    for h in range(2):
        ones2[h * PAD : h * PAD + WIN, h * HEAD : (h + 1) * HEAD] = 1.0
    ones2[0:WIN, 2 * HEAD :] = 1.0
    side_q = np.arange(PAD) >= WIN // 2
    side_k = np.arange(4 * PAD) % PAD >= WIN // 2
    far = np.where(side_q[:, None] != side_k[None, :], np.float32(FAR), np.float32(0.0))
    heads = np.zeros((16, 4, 128), np.float32)
    for h in range(4):
        heads[:, h, h * HEAD : (h + 1) * HEAD] = 1.0
    return dict(
        send1=np.stack(send1),
        gather1=np.stack(gather1),
        send2=send2,
        gather2=gather2,
        send3=send3,
        final=np.stack(final),
        ones4=ones4.astype(ml_dtypes.bfloat16),
        ones2=ones2.astype(ml_dtypes.bfloat16),
        far=far.astype(np.float32),
    )


ARGUMENTS = ("tokens", "norm_gain", "qkv_weight", "proj_weight", "merge_gain", "merge_weight", "coarse_gain", "coarse_qkv")
ARGUMENTS += ("coarse_proj", "up_weight", "up_gain", "out_weight")
TABLES = ("send1", "gather1", "send2", "gather2", "send3", "final", "ones4", "ones2", "far")


def dot(a, b):
    return jnp.dot(a, b, preferred_element_type=F32)


def norm(values, gain):
    average = jnp.mean(values, axis=-1, keepdims=True)
    centred = values - average
    spread = jnp.mean(centred * centred, axis=-1, keepdims=True)
    return (centred * lax.rsqrt(spread + EPSILON) * gain).astype(BF)


def attend(q, k, v, ones, masks, far):
    count = ones.shape[0] // PAD
    keys = jnp.concatenate([k * m for m in masks[:count]], axis=0)
    scores = lax.dot_general(q, keys, (((1,), (1,)), ((), ())), preferred_element_type=F32)
    if far is not None:
        scores = scores + far
    raised = jnp.exp2(scores).astype(BF)
    small = v * jnp.bfloat16(V_SCALE)
    values = jnp.concatenate([small * m for m in masks[:count]], axis=0)
    total = dot(raised, ones)
    return dot(raised, values) / (total * V_SCALE)


def kernel(lat_n, lon_n, *refs):
    names = list(ARGUMENTS)
    names += list(TABLES)
    hbm = dict(zip(names, refs))
    out_ref = refs[len(names)]
    scratch = refs[len(names) + 1 :]
    vm = dict(zip(names[1:], scratch))
    (qkv_pad, up_pad, far_v, buf1, buf2, buf3, snd1, snd2, snd3, load_sem, tok_sem, send_sem, recv_sem) = scratch[
        len(names) - 1 :
    ]

    lat, lon = lax.axis_index("lat"), lax.axis_index("lon")
    up, down = lax.rem(lat + 1, lat_n), lax.rem(lat + lat_n - 1, lat_n)
    east, west = lax.rem(lon + 1, lon_n), lax.rem(lon + lon_n - 1, lon_n)
    fore = ((up, lon), (lat, east), (up, east))
    back = ((down, lon), (lat, west), (down, west))

    barrier = pltpu.get_barrier_semaphore()
    for device in fore + back:
        pl.semaphore_signal(barrier, inc=1, device_id=device, device_id_type=MESH)

    loads = {}
    for level in range(2):
        loads["tokens", level] = pltpu.make_async_copy(
            hbm["tokens"].at[level], buf1.at[level, pl.ds(0, OWN)], tok_sem.at[level]
        )
        loads["tokens", level].start()
    order = ["send1", "gather1", "norm_gain", "qkv_weight", "ones4", "ones2", "far", "proj_weight", "send2", "gather2"]
    order += [n for n in names[1:] if n not in order]
    for i, n in enumerate(order):
        loads[n] = pltpu.make_async_copy(hbm[n], vm[n], load_sem.at[i])
        loads[n].start()

    def need(*wanted):
        for n in wanted:
            loads.pop(n).wait()

    def exchange(stage, level, source, target, starts, rows):
        forward = (level == 1) if stage < 2 else (level == 0)
        copies = []
        for i, device in enumerate(fore if forward else back):
            piece = pl.ds(starts[i][0], rows[i])
            place = pl.ds(starts[i][1], rows[i])
            copy = pltpu.make_async_remote_copy(
                src_ref=source.at[level, piece],
                dst_ref=target.at[level, place],
                send_sem=send_sem.at[stage, level, i],
                recv_sem=recv_sem.at[stage, level, i],
                device_id=device,
                device_id_type=MESH,
            )
            copy.start()
            copies.append(copy)
        return copies

    halo_rows = (64, 64, 32)

    def halo_starts(base):
        return ((LAT_AT, base + LAT_AT), (LON_AT, base + LON_AT), (DIAG_AT, base + DIAG_AT))

    need("send1")
    for level in range(2):
        need(("tokens", level))
        snd1[level] = dot(vm["send1"][level], buf1[level, 0:OWN]).astype(BF)
    pl.semaphore_wait(barrier, 6)
    one = [exchange(0, level, snd1, buf1, halo_starts(OWN), halo_rows) for level in range(2)]

    need("qkv_weight", "far")
    zero = jnp.zeros((C, 64), BF)
    for part in range(3):
        qkv_pad[:, part * 256 : part * 256 + C] = vm["qkv_weight"][:, part * C : (part + 1) * C]
        qkv_pad[:, part * 256 + C : (part + 1) * 256] = zero
    edge = (lat_n - 1, 0)
    for level in range(2):
        far_v[level] = jnp.where(lat == edge[level], vm["far"][...], 0.0)
    need("norm_gain", "ones4", "ones2", "proj_weight", "gather1")
    lane = lax.broadcasted_iota(jnp.int32, (PAD, 128), 1)
    masks = [jnp.where(lane // HEAD == h, 1.0, 0.0).astype(BF) for h in range(4)]
    ones4, ones2 = vm["ones4"], vm["ones2"]

    def fine(tokens, level, windows):
        normed = norm(tokens, vm["norm_gain"][...])
        packed = dot(normed, qkv_pad[...])
        q = (packed[:, 0:256] * Q_SCALE).astype(BF)
        k = packed[:, 256:512].astype(BF)
        v = packed[:, 512:768].astype(BF)
        heads = []
        for i, w in enumerate(windows):
            at = slice(i * PAD, (i + 1) * PAD)
            far = far_v[level[i]] if w >= 2 else None
            a = attend(q[at, 0:128], k[at, 0:128], v[at, 0:128], ones4[...], masks, far)
            far2 = far[:, 0 : 2 * PAD] if w >= 2 else None
            b = attend(q[at, 128:256], k[at, 128:256], v[at, 128:256], ones2[...], masks, far2)
            heads.append(jnp.concatenate([a, b], axis=1).astype(BF))
        heads = jnp.concatenate(heads, axis=0)[:, 0:C]
        result = (tokens + dot(heads, vm["proj_weight"][...])).astype(BF)
        for i, w in enumerate(windows):
            buf2[level[i], w * PAD : (w + 1) * PAD] = result[i * PAD : (i + 1) * PAD]

    first = [dot(vm["gather1"][level, 0:PAD, 0:OWN], buf1[level, 0:OWN]) for level in range(2)]
    fine(jnp.concatenate(first, axis=0), (0, 1), (0, 0))

    need("send2")
    two = []
    for level in range(2):
        for copy in one[level]:
            copy.wait_recv()
        rest = dot(vm["gather1"][level, PAD : 4 * PAD], buf1[level])
        fine(rest, (level,) * 3, (1, 2, 3))
        snd2[level] = dot(vm["send2"][...], buf2[level, 0 : 4 * PAD]).astype(BF)
        two.append(exchange(1, level, snd2, buf2, halo_starts(4 * PAD), halo_rows))

    need("up_weight")
    for k in range(4):
        up_pad[:, k * 256 : k * 256 + C] = vm["up_weight"][:, k * C : (k + 1) * C]
    need("gather2", "send3", "merge_gain", "merge_weight", "coarse_gain", "coarse_qkv", "coarse_proj")
    need("up_gain", "out_weight", "final")

    three = []
    for level in range(2):
        for copy in two[level]:
            copy.wait_recv()
        cells = dot(vm["gather2"][...], buf2[level])
        group = [cells[k * PAD : (k + 1) * PAD] for k in range(4)]
        column = [k if level == 0 else 3 - k for k in range(4)]
        average = jnp.sum(group[0] + group[1] + group[2] + group[3], axis=-1, keepdims=True) * (1.0 / (4 * C))
        centred = [g - average for g in group]
        squares = [c * c for c in centred]
        spread = jnp.sum(squares[0] + squares[1] + squares[2] + squares[3], axis=-1, keepdims=True) * (1.0 / (4 * C))
        scale = lax.rsqrt(spread + EPSILON)
        coarse = jnp.zeros((PAD, CC), F32)
        for k in range(4):
            stacked = (centred[k] * scale * vm["merge_gain"][column[k] : column[k] + 1]).astype(BF)
            coarse = coarse + dot(stacked, vm["merge_weight"][column[k] * C : (column[k] + 1) * C])
        coarse = coarse.astype(BF).astype(F32)
        normed = norm(coarse, vm["coarse_gain"][...])
        packed = dot(normed, vm["coarse_qkv"][...])
        heads = []
        for j in range(3):
            q = (packed[:, j * 128 : (j + 1) * 128] * Q_SCALE).astype(BF)
            k = packed[:, CC + j * 128 : CC + (j + 1) * 128].astype(BF)
            v = packed[:, 2 * CC + j * 128 : 2 * CC + (j + 1) * 128].astype(BF)
            heads.append(attend(q, k, v, ones4[...], masks, far_v[level]).astype(BF))
        heads = jnp.concatenate(heads, axis=1)
        coarse_out = (coarse + dot(heads, vm["coarse_proj"][...])).astype(BF)
        normed = []
        for k in range(4):
            lifted = dot(coarse_out, up_pad[:, column[k] * 256 : column[k] * 256 + C])
            normed.append(norm(lifted, vm["up_gain"][...]))
        branch = dot(jnp.concatenate(normed, axis=0), vm["out_weight"][...])
        encoded = (cells + branch).astype(BF)
        quarters = dot(vm["send3"][...], encoded).astype(BF)
        buf3[level, 0:PAD] = quarters[0:PAD]
        snd3[level] = quarters[PAD : 4 * PAD]
        places = ((PAD, 2 * PAD), (0, PAD), (2 * PAD, 3 * PAD))
        three.append(exchange(2, level, snd3, buf3, places, (PAD, PAD, PAD)))

    for level in range(2):
        for copy in three[level]:
            copy.wait_recv()
        out_ref[level] = dot(vm["final"][level], buf3[level]).astype(BF)
    for copies in one + two + three:
        for copy in copies:
            copy.wait_send()


def body(lat_n, lon_n, tokens, norm_gain, qkv_weight, proj_weight, merge_gain, merge_weight, coarse_gain, *rest):
    coarse_qkv, coarse_proj, up_weight, up_gain, out_weight = rest
    table = tables()
    args = [
        tokens.reshape(2, OWN, C),
        norm_gain.reshape(1, C),
        qkv_weight,
        proj_weight,
        merge_gain.reshape(4, C),
        merge_weight,
        coarse_gain.reshape(1, CC),
        coarse_qkv,
        coarse_proj,
        up_weight,
        up_gain.reshape(1, C),
        out_weight,
    ] + [jnp.asarray(table[n]) for n in TABLES]
    scratch = [pltpu.VMEM(a.shape, a.dtype) for a in args[1:]]
    scratch += [
        pltpu.VMEM((C, 768), BF),
        pltpu.VMEM((CC, 1024), BF),
        pltpu.VMEM((2, PAD, 4 * PAD), F32),
        pltpu.VMEM((2, OWN + HALO, C), BF),
        pltpu.VMEM((2, 4 * PAD + HALO, C), BF),
        pltpu.VMEM((2, 4 * PAD, C), BF),
        pltpu.VMEM((2, HALO, C), BF),
        pltpu.VMEM((2, HALO, C), BF),
        pltpu.VMEM((2, 3 * PAD, C), BF),
        pltpu.SemaphoreType.DMA((len(args) - 1,)),
        pltpu.SemaphoreType.DMA((2,)),
        pltpu.SemaphoreType.DMA((3, 2, 3)),
        pltpu.SemaphoreType.DMA((3, 2, 3)),
    ]
    out = pl.pallas_call(
        functools.partial(kernel, lat_n, lon_n),
        out_shape=jax.ShapeDtypeStruct((2, OWN, C), BF),
        in_specs=[pl.BlockSpec(memory_space=pl.ANY)] * len(args),
        out_specs=pl.BlockSpec(memory_space=pltpu.VMEM),
        scratch_shapes=scratch,
        compiler_params=pltpu.CompilerParams(
            collective_id=0, has_side_effects=True, vmem_limit_bytes=48 * 1024 * 1024
        ),
    )(*args)
    return out.reshape(tokens.shape)


def solution(mesh):
    placed = (P(None, "lat", "lon", None),) + (P(),) * 11
    return jax.shard_map(
        functools.partial(body, mesh.shape["lat"], mesh.shape["lon"]),
        mesh=mesh,
        in_specs=placed,
        out_specs=P(None, "lat", "lon", None),
        check_vma=False,
    )
```

```python
import functools

import jax
import jax.numpy as jnp
import ml_dtypes
import numpy as np
from jax import lax
from jax.experimental import pallas as pl
from jax.experimental.pallas import tpu as pltpu
from jax.sharding import PartitionSpec as P

MESH = pl.DeviceIdType.MESH
BF = jnp.bfloat16
F32 = jnp.float32
EPSILON = 1e-05
C = 192
CC = 384
ROWS, COLS = 12, 24
OWN = ROWS * COLS
UNIT = 18
WIN = 72
PAD = 80
HEAD = 32
Q_SCALE = float(HEAD**-0.5 * np.log2(np.e))
V_SCALE = 2.0**-8
FAR = -1e30
HALO = 160
LAT_AT, LON_AT, DIAG_AT = 0, 64, 128


def one_hot(rows, cols, pairs):
    out = np.zeros((rows, cols), np.float32)
    for r, c in pairs:
        out[r, c] = 1.0
    return out.astype(ml_dtypes.bfloat16)


def halo_slot(unit_of):
    for j in range(3):
        yield LAT_AT + j * UNIT, (0, j + 1)
        yield LON_AT + j * UNIT, (j + 1, 0)
    yield DIAG_AT, (0, 0)


def received(a, b):
    if a == 3 and b == 3:
        return DIAG_AT
    if a == 3:
        return LAT_AT + b * UNIT
    if b == 3:
        return LON_AT + a * UNIT
    return None


def window_row(a, b):
    return ((a // 2) * 2 + b // 2) * PAD + ((a % 2) * 2 + b % 2) * UNIT


def natural(level, r, c):
    n = r * COLS + c
    return n if level == 0 else OWN - 1 - n


@functools.cache
def tables():
    units = [(a, b) for a in range(4) for b in range(4)]
    send1, gather1, final = [], [], []
    for level in range(2):

        def own(a, b, t, level=level):
            return natural(level, a * 3 + t // 6, b * 6 + t % 6)

        send1.append(
            one_hot(HALO, OWN, [(s + t, own(a, b, t)) for s, (a, b) in halo_slot(None) for t in range(UNIT)])
        )
        pairs = []
        for a, b in units:
            slot = received(a, b)
            for t in range(UNIT):
                source = own(a + 1, b + 1, t) if slot is None else OWN + slot + t
                pairs.append((window_row(a, b) + t, source))
        gather1.append(one_hot(4 * PAD, OWN + HALO, pairs))
        pairs = []
        for r in range(ROWS):
            for c in range(COLS):
                qr, qc = int(r < 6), int(c < 12)
                y, x = r % 6, c % 12
                k = y % 2 + 2 * (x % 2)
                t = (y // 2) * 6 + x // 2
                pairs.append((natural(level, r, c), (qr * 2 + qc) * PAD + k * UNIT + t))
        final.append(one_hot(OWN, 4 * PAD, pairs))
    send2 = one_hot(
        HALO, 4 * PAD, [(s + t, window_row(a, b) + t) for s, (a, b) in halo_slot(None) for t in range(UNIT)]
    )
    pairs = []
    for y in range(ROWS):
        for x in range(COLS):
            a, b, t = y // 3, x // 6, (y % 3) * 6 + x % 6
            slot = received(a, b)
            source = window_row(a + 1, b + 1) + t if slot is None else 4 * PAD + slot + t
            k = y % 2 + 2 * (x % 2)
            i, j = y // 2, x // 2
            cell = ((i // 3) * 2 + j // 6) * UNIT + (i % 3) * 6 + j % 6
            pairs.append((k * PAD + cell, source))
    gather2 = one_hot(4 * PAD, 4 * PAD + HALO, pairs)
    pairs = []
    for quarter in range(4):
        for k in range(4):
            for t in range(UNIT):
                pairs.append((quarter * PAD + k * UNIT + t, k * PAD + quarter * UNIT + t))
    send3 = one_hot(4 * PAD, 4 * PAD, pairs)
    ones4 = np.zeros((4 * PAD, 128), np.float32)
    ones2 = np.zeros((2 * PAD, 128), np.float32)
    for h in range(4):
        ones4[h * PAD : h * PAD + WIN, h * HEAD : (h + 1) * HEAD] = 1.0
    for h in range(2):
        ones2[h * PAD : h * PAD + WIN, h * HEAD : (h + 1) * HEAD] = 1.0
    ones2[0:WIN, 2 * HEAD :] = 1.0
    side_q = np.arange(PAD) >= WIN // 2
    side_k = np.arange(4 * PAD) % PAD >= WIN // 2
    far = np.where(side_q[:, None] != side_k[None, :], np.float32(FAR), np.float32(0.0))
    heads = np.zeros((16, 4, 128), np.float32)
    for h in range(4):
        heads[:, h, h * HEAD : (h + 1) * HEAD] = 1.0
    return dict(
        send1=np.stack(send1),
        gather1=np.stack(gather1),
        send2=send2,
        gather2=gather2,
        send3=send3,
        final=np.stack(final),
        ones4=ones4.astype(ml_dtypes.bfloat16),
        ones2=ones2.astype(ml_dtypes.bfloat16),
        far=far.astype(np.float32),
    )


ARGUMENTS = ("tokens", "norm_gain", "qkv_weight", "proj_weight", "merge_gain", "merge_weight", "coarse_gain", "coarse_qkv")
ARGUMENTS += ("coarse_proj", "up_weight", "up_gain", "out_weight")
TABLES = ("send1", "gather1", "send2", "gather2", "send3", "final", "ones4", "ones2", "far")


def dot(a, b):
    return jnp.dot(a, b, preferred_element_type=F32)


def norm(values, gain):
    average = jnp.mean(values, axis=-1, keepdims=True)
    centred = values - average
    spread = jnp.mean(centred * centred, axis=-1, keepdims=True)
    return (centred * lax.rsqrt(spread + EPSILON) * gain).astype(BF)


def attend(q, k, v, ones, masks, far):
    count = ones.shape[0] // PAD
    keys = jnp.concatenate([k * m for m in masks[:count]], axis=0)
    scores = lax.dot_general(q, keys, (((1,), (1,)), ((), ())), preferred_element_type=F32)
    if far is not None:
        scores = scores + far
    raised = jnp.exp2(scores).astype(BF)
    small = v * jnp.bfloat16(V_SCALE)
    values = jnp.concatenate([small * m for m in masks[:count]], axis=0)
    total = dot(raised, ones)
    return dot(raised, values) / (total * V_SCALE)


def kernel(lat_n, lon_n, *refs):
    names = list(ARGUMENTS)
    names += list(TABLES)
    hbm = dict(zip(names, refs))
    out_ref = refs[len(names)]
    scratch = refs[len(names) + 1 :]
    vm = dict(zip(names[1:], scratch))
    (qkv_pad, up_pad, far_v, buf1, buf2, buf3, snd1, snd2, snd3, load_sem, tok_sem, send_sem, recv_sem) = scratch[
        len(names) - 1 :
    ]

    lat, lon = lax.axis_index("lat"), lax.axis_index("lon")
    up, down = lax.rem(lat + 1, lat_n), lax.rem(lat + lat_n - 1, lat_n)
    east, west = lax.rem(lon + 1, lon_n), lax.rem(lon + lon_n - 1, lon_n)
    fore = ((up, lon), (lat, east), (up, east))
    back = ((down, lon), (lat, west), (down, west))

    barrier = pltpu.get_barrier_semaphore()
    for device in fore + back:
        pl.semaphore_signal(barrier, inc=1, device_id=device, device_id_type=MESH)

    loads = {}
    for level in range(2):
        loads["tokens", level] = pltpu.make_async_copy(
            hbm["tokens"].at[level], buf1.at[level, pl.ds(0, OWN)], tok_sem.at[level]
        )
        loads["tokens", level].start()
    order = ["send1", "gather1", "norm_gain", "qkv_weight", "ones4", "ones2", "far", "proj_weight", "send2", "gather2"]
    order += [n for n in names[1:] if n not in order]
    for i, n in enumerate(order):
        loads[n] = pltpu.make_async_copy(hbm[n], vm[n], load_sem.at[i])
        loads[n].start()

    def need(*wanted):
        for n in wanted:
            loads.pop(n).wait()

    def row(n):
        return vm[n][...].reshape(1, -1)

    def exchange(stage, level, source, target, starts, rows):
        forward = (level == 1) if stage < 2 else (level == 0)
        copies = []
        for i, device in enumerate(fore if forward else back):
            piece = pl.ds(starts[i][0], rows[i])
            place = pl.ds(starts[i][1], rows[i])
            copy = pltpu.make_async_remote_copy(
                src_ref=source.at[level, piece],
                dst_ref=target.at[level, place],
                send_sem=send_sem.at[stage, level, i],
                recv_sem=recv_sem.at[stage, level, i],
                device_id=device,
                device_id_type=MESH,
            )
            copy.start()
            copies.append(copy)
        return copies

    halo_rows = (64, 64, 32)

    def halo_starts(base):
        return ((LAT_AT, base + LAT_AT), (LON_AT, base + LON_AT), (DIAG_AT, base + DIAG_AT))

    need("send1")
    for level in range(2):
        need(("tokens", level))
        snd1[level] = dot(vm["send1"][level], buf1[level, 0:OWN]).astype(BF)
    pl.semaphore_wait(barrier, 6)
    one = [exchange(0, level, snd1, buf1, halo_starts(OWN), halo_rows) for level in range(2)]

    need("qkv_weight", "far")
    zero = jnp.zeros((C, 64), BF)
    for part in range(3):
        qkv_pad[:, part * 256 : part * 256 + C] = vm["qkv_weight"][:, part * C : (part + 1) * C]
        qkv_pad[:, part * 256 + C : (part + 1) * 256] = zero
    edge = (lat_n - 1, 0)
    for level in range(2):
        far_v[level] = jnp.where(lat == edge[level], vm["far"][...], 0.0)
    need("norm_gain", "ones4", "ones2", "proj_weight", "gather1")
    lane = lax.broadcasted_iota(jnp.int32, (PAD, 128), 1)
    masks = [jnp.where(lane // HEAD == h, 1.0, 0.0).astype(BF) for h in range(4)]
    ones4, ones2 = vm["ones4"], vm["ones2"]

    def fine(tokens, level, windows):
        normed = norm(tokens, row("norm_gain"))
        packed = dot(normed, qkv_pad[...])
        q = (packed[:, 0:256] * Q_SCALE).astype(BF)
        k = packed[:, 256:512].astype(BF)
        v = packed[:, 512:768].astype(BF)
        heads = []
        for i, w in enumerate(windows):
            at = slice(i * PAD, (i + 1) * PAD)
            far = far_v[level[i]] if w >= 2 else None
            a = attend(q[at, 0:128], k[at, 0:128], v[at, 0:128], ones4[...], masks, far)
            far2 = far[:, 0 : 2 * PAD] if w >= 2 else None
            b = attend(q[at, 128:256], k[at, 128:256], v[at, 128:256], ones2[...], masks, far2)
            heads.append(jnp.concatenate([a, b], axis=1).astype(BF))
        heads = jnp.concatenate(heads, axis=0)[:, 0:C]
        result = (tokens + dot(heads, vm["proj_weight"][...])).astype(BF)
        for i, w in enumerate(windows):
            buf2[level[i], w * PAD : (w + 1) * PAD] = result[i * PAD : (i + 1) * PAD]

    first = [dot(vm["gather1"][level, 0:PAD, 0:OWN], buf1[level, 0:OWN]) for level in range(2)]
    fine(jnp.concatenate(first, axis=0), (0, 1), (0, 0))

    need("send2")
    two = []
    for level in range(2):
        for copy in one[level]:
            copy.wait_recv()
        rest = dot(vm["gather1"][level, PAD : 4 * PAD], buf1[level])
        fine(rest, (level,) * 3, (1, 2, 3))
        snd2[level] = dot(vm["send2"][...], buf2[level, 0 : 4 * PAD]).astype(BF)
        two.append(exchange(1, level, snd2, buf2, halo_starts(4 * PAD), halo_rows))

    need("up_weight")
    for k in range(4):
        up_pad[:, k * 256 : k * 256 + C] = vm["up_weight"][:, k * C : (k + 1) * C]
    need("gather2", "send3", "merge_gain", "merge_weight", "coarse_gain", "coarse_qkv", "coarse_proj")
    need("up_gain", "out_weight", "final")

    three = []
    for level in range(2):
        for copy in two[level]:
            copy.wait_recv()
        cells = dot(vm["gather2"][...], buf2[level])
        group = [cells[k * PAD : (k + 1) * PAD] for k in range(4)]
        column = [k if level == 0 else 3 - k for k in range(4)]
        average = jnp.sum(group[0] + group[1] + group[2] + group[3], axis=-1, keepdims=True) * (1.0 / (4 * C))
        centred = [g - average for g in group]
        squares = [c * c for c in centred]
        spread = jnp.sum(squares[0] + squares[1] + squares[2] + squares[3], axis=-1, keepdims=True) * (1.0 / (4 * C))
        scale = lax.rsqrt(spread + EPSILON)
        coarse = jnp.zeros((PAD, CC), F32)
        for k in range(4):
            stacked = (centred[k] * scale * row("merge_gain")[:, column[k] * C : (column[k] + 1) * C]).astype(BF)
            coarse = coarse + dot(stacked, vm["merge_weight"][column[k] * C : (column[k] + 1) * C])
        coarse = coarse.astype(BF).astype(F32)
        normed = norm(coarse, row("coarse_gain"))
        packed = dot(normed, vm["coarse_qkv"][...])
        heads = []
        for j in range(3):
            q = (packed[:, j * 128 : (j + 1) * 128] * Q_SCALE).astype(BF)
            k = packed[:, CC + j * 128 : CC + (j + 1) * 128].astype(BF)
            v = packed[:, 2 * CC + j * 128 : 2 * CC + (j + 1) * 128].astype(BF)
            heads.append(attend(q, k, v, ones4[...], masks, far_v[level]).astype(BF))
        heads = jnp.concatenate(heads, axis=1)
        coarse_out = (coarse + dot(heads, vm["coarse_proj"][...])).astype(BF)
        normed = []
        for k in range(4):
            lifted = dot(coarse_out, up_pad[:, column[k] * 256 : column[k] * 256 + C])
            normed.append(norm(lifted, row("up_gain")))
        branch = dot(jnp.concatenate(normed, axis=0), vm["out_weight"][...])
        encoded = (cells + branch).astype(BF)
        quarters = dot(vm["send3"][...], encoded).astype(BF)
        buf3[level, 0:PAD] = quarters[0:PAD]
        snd3[level] = quarters[PAD : 4 * PAD]
        places = ((PAD, 2 * PAD), (0, PAD), (2 * PAD, 3 * PAD))
        three.append(exchange(2, level, snd3, buf3, places, (PAD, PAD, PAD)))

    for level in range(2):
        for copy in three[level]:
            copy.wait_recv()
        out_ref[level] = dot(vm["final"][level], buf3[level]).astype(BF)
    for copies in one + two + three:
        for copy in copies:
            copy.wait_send()


def body(lat_n, lon_n, tokens, norm_gain, qkv_weight, proj_weight, merge_gain, merge_weight, coarse_gain, *rest):
    coarse_qkv, coarse_proj, up_weight, up_gain, out_weight = rest
    table = tables()
    args = [
        tokens.reshape(2, OWN, C),
        norm_gain,
        qkv_weight,
        proj_weight,
        merge_gain,
        merge_weight,
        coarse_gain,
        coarse_qkv,
        coarse_proj,
        up_weight,
        up_gain,
        out_weight,
    ] + [jnp.asarray(table[n]) for n in TABLES]
    scratch = [pltpu.VMEM(a.shape, a.dtype) for a in args[1:]]
    scratch += [
        pltpu.VMEM((C, 768), BF),
        pltpu.VMEM((CC, 1024), BF),
        pltpu.VMEM((2, PAD, 4 * PAD), F32),
        pltpu.VMEM((2, OWN + HALO, C), BF),
        pltpu.VMEM((2, 4 * PAD + HALO, C), BF),
        pltpu.VMEM((2, 4 * PAD, C), BF),
        pltpu.VMEM((2, HALO, C), BF),
        pltpu.VMEM((2, HALO, C), BF),
        pltpu.VMEM((2, 3 * PAD, C), BF),
        pltpu.SemaphoreType.DMA((len(args) - 1,)),
        pltpu.SemaphoreType.DMA((2,)),
        pltpu.SemaphoreType.DMA((3, 2, 3)),
        pltpu.SemaphoreType.DMA((3, 2, 3)),
    ]
    out = pl.pallas_call(
        functools.partial(kernel, lat_n, lon_n),
        out_shape=jax.ShapeDtypeStruct((2, OWN, C), BF),
        in_specs=[pl.BlockSpec(memory_space=pltpu.HBM)] * len(args),
        out_specs=pl.BlockSpec(memory_space=pltpu.VMEM),
        scratch_shapes=scratch,
        compiler_params=pltpu.CompilerParams(
            collective_id=0, has_side_effects=True, vmem_limit_bytes=40 * 1024 * 1024
        ),
    )(*[pltpu.with_memory_space_constraint(a, pltpu.HBM) for a in args])
    return out.reshape(tokens.shape)


def solution(mesh):
    placed = (P(None, "lat", "lon", None),) + (P(),) * 11
    return jax.shard_map(
        functools.partial(body, mesh.shape["lat"], mesh.shape["lon"]),
        mesh=mesh,
        in_specs=placed,
        out_specs=P(None, "lat", "lon", None),
        check_vma=False,
    )
```

```python
import functools

import jax
import jax.numpy as jnp
import ml_dtypes
import numpy as np
from jax import lax
from jax.experimental import pallas as pl
from jax.experimental.pallas import tpu as pltpu
from jax.sharding import PartitionSpec as P

MESH = pl.DeviceIdType.MESH
BF = jnp.bfloat16
F32 = jnp.float32
EPSILON = 1e-05
C = 192
CC = 384
ROWS, COLS = 12, 24
OWN = ROWS * COLS
UNIT = 18
WIN = 72
PAD = 80
HEAD = 32
Q_SCALE = float(HEAD**-0.5 * np.log2(np.e))
V_SCALE = 2.0**-8
FAR = -1e30
HALO = 160
LAT_AT, LON_AT, DIAG_AT = 0, 64, 128
HALO2 = 208
RESULTS = (
    (0, 4 * PAD, 32, 2),
    (16, 4 * PAD + 32, 32, 0),
    (32, 4 * PAD + 64, 32, 1),
    (PAD, 4 * PAD + 96, 48, 0),
    (2 * PAD, 4 * PAD + 144, 64, 1),
)
TOKENS = ((DIAG_AT, OWN + DIAG_AT, 32, 2), (LAT_AT, OWN + LAT_AT, 64, 0), (LON_AT, OWN + LON_AT, 64, 1))
ENCODED = ((2 * PAD, 3 * PAD, PAD, 2), (PAD, 2 * PAD, PAD, 0), (0, PAD, PAD, 1))


def one_hot(rows, cols, pairs):
    out = np.zeros((rows, cols), np.float32)
    for r, c in pairs:
        out[r, c] = 1.0
    return out.astype(ml_dtypes.bfloat16)


def halo_slot():
    for j in range(3):
        yield LAT_AT + j * UNIT, (0, j + 1)
        yield LON_AT + j * UNIT, (j + 1, 0)
    yield DIAG_AT, (0, 0)


def received(a, b):
    if a == 3 and b == 3:
        return DIAG_AT
    if a == 3:
        return LAT_AT + b * UNIT
    if b == 3:
        return LON_AT + a * UNIT
    return None


def window_row(a, b):
    return ((a // 2) * 2 + b // 2) * PAD + ((a % 2) * 2 + b % 2) * UNIT


def arrival(a, b):
    if a < 3 and b < 3:
        return window_row(a + 1, b + 1)
    which = {(3, 0): 1, (3, 1): 3, (3, 2): 3, (0, 3): 2, (1, 3): 4, (2, 3): 4, (3, 3): 0}[a, b]
    theirs = window_row(0 if a == 3 else a + 1, 0 if b == 3 else b + 1)
    return RESULTS[which][1] + theirs - RESULTS[which][0]


def natural(level, r, c):
    n = r * COLS + c
    return n if level == 0 else OWN - 1 - n


@functools.cache
def tables():
    units = [(a, b) for a in range(4) for b in range(4)]
    send1, gather1, final = [], [], []
    for level in range(2):

        def own(a, b, t, level=level):
            return natural(level, a * 3 + t // 6, b * 6 + t % 6)

        send1.append(
            one_hot(HALO, OWN, [(s + t, own(a, b, t)) for s, (a, b) in halo_slot() for t in range(UNIT)])
        )
        pairs = []
        for a, b in units:
            slot = received(a, b)
            for t in range(UNIT):
                source = own(a + 1, b + 1, t) if slot is None else OWN + slot + t
                pairs.append((window_row(a, b) + t, source))
        gather1.append(one_hot(4 * PAD, OWN + HALO, pairs))
        pairs = []
        for r in range(ROWS):
            for c in range(COLS):
                qr, qc = int(r < 6), int(c < 12)
                y, x = r % 6, c % 12
                k = y % 2 + 2 * (x % 2)
                t = (y // 2) * 6 + x // 2
                pairs.append((natural(level, r, c), (qr * 2 + qc) * PAD + k * UNIT + t))
        final.append(one_hot(OWN, 4 * PAD, pairs))
    pairs = []
    for y in range(ROWS):
        for x in range(COLS):
            a, b, t = y // 3, x // 6, (y % 3) * 6 + x % 6
            source = arrival(a, b) + t
            k = y % 2 + 2 * (x % 2)
            i, j = y // 2, x // 2
            cell = ((i // 3) * 2 + j // 6) * UNIT + (i % 3) * 6 + j % 6
            pairs.append((k * PAD + cell, source))
    gather2 = one_hot(4 * PAD, 4 * PAD + HALO2, pairs)
    pairs = []
    for quarter in range(4):
        for k in range(4):
            for t in range(UNIT):
                pairs.append((quarter * PAD + k * UNIT + t, k * PAD + quarter * UNIT + t))
    send3 = one_hot(4 * PAD, 4 * PAD, pairs)
    ones4 = np.zeros((4 * PAD, 128), np.float32)
    ones2 = np.zeros((224, 128), np.float32)
    for h in range(4):
        ones4[h * PAD : h * PAD + WIN, h * HEAD : (h + 1) * HEAD] = 1.0
    for h in range(2):
        ones2[64 + h * PAD : 64 + h * PAD + WIN, h * HEAD : (h + 1) * HEAD] = 1.0
    ones2[64 : 64 + WIN, 2 * HEAD :] = 1.0
    side_q = np.arange(PAD) >= WIN // 2
    side_k = np.arange(6 * PAD) % PAD >= WIN // 2
    far = np.where(side_q[:, None] != side_k[None, :], np.float32(FAR), np.float32(0.0))
    return dict(
        send1=np.stack(send1),
        gather1=np.stack(gather1),
        gather2=gather2,
        send3=send3,
        final=np.stack(final),
        ones4=ones4.astype(ml_dtypes.bfloat16),
        ones2=ones2.astype(ml_dtypes.bfloat16),
        far=far.astype(np.float32),
    )


ARGUMENTS = ("tokens", "norm_gain", "qkv_weight", "proj_weight", "merge_gain", "merge_weight", "coarse_gain", "coarse_qkv")
ARGUMENTS += ("coarse_proj", "up_weight", "up_gain", "out_weight")
EARLY = ("send1", "norm_gain", "qkv_weight", "far", "ones4", "ones2", "proj_weight", "gather1")
TABLES = ("send1", "gather1", "gather2", "send3", "final", "ones4", "ones2", "far")


def dot(a, b):
    return jnp.dot(a, b, preferred_element_type=F32)


def centre(values, gain):
    centred = values - jnp.mean(values, axis=-1, keepdims=True)
    spread = jnp.mean(centred * centred, axis=-1, keepdims=True)
    return (centred * gain).astype(BF), lax.rsqrt(spread + EPSILON)


def dot_t(a, b):
    return lax.dot_general(a, b, (((1,), (1,)), ((), ())), preferred_element_type=F32)


def shared(raised, values, ones):
    both = dot(raised, jnp.concatenate([values, ones], axis=1))
    return both[:, 0:128] / (both[:, 128:256] * V_SCALE)


def attend4(q, k, v, ones4, masks, far):
    keys = jnp.concatenate([k * m for m in masks], axis=0)
    raised = jnp.exp2(dot_t(q, keys) + far).astype(BF)
    small = v * jnp.bfloat16(V_SCALE)
    return shared(raised, jnp.concatenate([small * m for m in masks], axis=0), ones4)


def attend6(q, k, v, ones4, ones2, masks, far):
    zero = jnp.zeros((PAD, 128), BF)
    k0, k1 = k[:, 0:128], k[:, 128:256]
    keys = [jnp.concatenate([k0 * m, zero], axis=1) for m in masks]
    keys += [jnp.concatenate([zero, k1 * m], axis=1) for m in masks[0:2]]
    scores = dot_t(q, jnp.concatenate(keys, axis=0))
    if far is not None:
        scores = scores + far
    raised = jnp.exp2(scores).astype(BF)
    small = v * jnp.bfloat16(V_SCALE)
    v0, v1 = small[:, 0:128], small[:, 128:256]
    first = shared(raised[:, 0 : 4 * PAD], jnp.concatenate([v0 * m for m in masks], axis=0), ones4)
    last = [zero[0:64]] + [v1 * m for m in masks[0:2]]
    last = shared(raised[:, 256 : 6 * PAD], jnp.concatenate(last, axis=0), ones2)
    return jnp.concatenate([first, last], axis=1).astype(BF)


def kernel(lat_n, lon_n, *refs):
    names = list(ARGUMENTS)
    names += list(TABLES)
    hbm = dict(zip(names, refs))
    out_ref = refs[len(names)]
    scratch = refs[len(names) + 1 :]
    vm = dict(zip(names[1:], scratch))
    (qkv_pad, up_pad, far_v, buf1, buf2, buf3, snd1, snd3, load_sem, tok_sem, send_sem, recv_sem) = scratch[
        len(names) - 1 :
    ]

    lat, lon = lax.axis_index("lat"), lax.axis_index("lon")
    up, down = lax.rem(lat + 1, lat_n), lax.rem(lat + lat_n - 1, lat_n)
    east, west = lax.rem(lon + 1, lon_n), lax.rem(lon + lon_n - 1, lon_n)
    fore = ((up, lon), (lat, east), (up, east))
    back = ((down, lon), (lat, west), (down, west))

    barrier = pltpu.get_barrier_semaphore()
    for device in fore + back:
        pl.semaphore_signal(barrier, inc=1, device_id=device, device_id_type=MESH)

    loads = {}
    for level in range(2):
        loads["tokens", level] = pltpu.make_async_copy(
            hbm["tokens"].at[level], buf1.at[level, pl.ds(0, OWN)], tok_sem.at[level]
        )
        loads["tokens", level].start()
    order = ["send1"] + [n for n in EARLY if n != "send1"]
    order += [n for n in names[1:] if n not in order]

    def load(*wanted):
        for n in wanted:
            loads[n] = pltpu.make_async_copy(hbm[n], vm[n], load_sem.at[order.index(n)])
            loads[n].start()

    load("send1")

    def need(*wanted):
        for n in wanted:
            loads.pop(n).wait()

    def row(n):
        return vm[n][...].reshape(1, -1)

    def send(stage, level, which, source, target, plan):
        forward = (level == 1) if stage < 2 else (level == 0)
        copies = {}
        for i in which:
            start, place, rows, neighbour = plan[i]
            copies[i] = pltpu.make_async_remote_copy(
                src_ref=source.at[level, pl.ds(start, rows)],
                dst_ref=target.at[level, pl.ds(place, rows)],
                send_sem=send_sem.at[stage, level, i],
                recv_sem=recv_sem.at[stage, level, i],
                device_id=(fore if forward else back)[neighbour],
                device_id_type=MESH,
            )
            copies[i].start()
        return copies

    need("send1")
    for level in range(2):
        need(("tokens", level))
        snd1[level] = dot(vm["send1"][level], buf1[level, 0:OWN]).astype(BF)
    pl.semaphore_wait(barrier, 6)
    one = [send(0, level, (0, 1, 2), snd1, buf1, TOKENS) for level in range(2)]
    load(*order[1:])

    need("qkv_weight", "far")
    zero = jnp.zeros((C, 64), BF)
    for part in range(3):
        qkv_pad[:, part * 256 : part * 256 + C] = vm["qkv_weight"][:, part * C : (part + 1) * C]
        qkv_pad[:, part * 256 + C : (part + 1) * 256] = zero
    edge = (lat_n - 1, 0)
    for level in range(2):
        far_v[level] = jnp.where(lat == edge[level], vm["far"][...], 0.0)
    need("norm_gain", "ones4", "ones2", "proj_weight", "gather1")
    lane = lax.broadcasted_iota(jnp.int32, (PAD, 128), 1)
    masks = [jnp.where(lane // HEAD == h, 1.0, 0.0).astype(BF) for h in range(4)]
    ones4, ones2 = vm["ones4"], vm["ones2"]

    def fine(tokens, items):
        normed, scale = centre(tokens, row("norm_gain"))
        packed = dot(normed, qkv_pad[...]) * scale
        q = (packed[:, 0:256] * Q_SCALE).astype(BF)
        k = packed[:, 256:512].astype(BF)
        v = packed[:, 512:768].astype(BF)
        heads = []
        for i, (level, w) in enumerate(items):
            at = slice(i * PAD, (i + 1) * PAD)
            far = far_v[level] if w >= 2 else None
            heads.append(attend6(q[at], k[at], v[at], ones4[...], ones2[...], masks, far))
        heads = jnp.concatenate(heads, axis=0)[:, 0:C]
        result = (tokens + dot(heads, vm["proj_weight"][...])).astype(BF)
        for i, (level, w) in enumerate(items):
            buf2[level, w * PAD : (w + 1) * PAD] = result[i * PAD : (i + 1) * PAD]

    first = [dot(vm["gather1"][level, 0:PAD, 0:OWN], buf1[level, 0:OWN]) for level in range(2)]
    fine(jnp.concatenate(first, axis=0), [(0, 0), (1, 0)])

    two = [send(1, level, (0, 1, 2), buf2, buf2, RESULTS) for level in range(2)]

    for level in range(2):
        one[level][1].wait_recv()
        one[level][2].wait_recv()
    near = OWN + DIAG_AT
    rest = [dot(vm["gather1"][level, PAD : 3 * PAD, 0:near], buf1[level, 0:near]) for level in range(2)]
    fine(jnp.concatenate(rest, axis=0), [(0, 1), (0, 2), (1, 1), (1, 2)])
    for level in range(2):
        two[level].update(send(1, level, (3, 4), buf2, buf2, RESULTS))
    for level in range(2):
        one[level][0].wait_recv()
    last = [dot(vm["gather1"][level, 3 * PAD : 4 * PAD], buf1[level]) for level in range(2)]
    fine(jnp.concatenate(last, axis=0), [(0, 3), (1, 3)])

    need("up_weight")
    for k in range(4):
        up_pad[:, k * 256 : k * 256 + C] = vm["up_weight"][:, k * C : (k + 1) * C]
    need("gather2", "send3", "merge_gain", "merge_weight", "coarse_gain", "coarse_qkv", "coarse_proj")
    need("up_gain", "out_weight", "final")

    for level in range(2):
        for copy in two[level].values():
            copy.wait_recv()
    cells = [dot(vm["gather2"][...], buf2[level]) for level in range(2)]
    group = [
        jnp.concatenate([cells[0][k * PAD : (k + 1) * PAD], cells[1][(3 - k) * PAD : (4 - k) * PAD]], axis=0)
        for k in range(4)
    ]
    average = jnp.sum(group[0] + group[1] + group[2] + group[3], axis=-1, keepdims=True) * (1.0 / (4 * C))
    centred = [g - average for g in group]
    squares = [c * c for c in centred]
    spread = jnp.sum(squares[0] + squares[1] + squares[2] + squares[3], axis=-1, keepdims=True) * (1.0 / (4 * C))
    scale = lax.rsqrt(spread + EPSILON)
    coarse = jnp.zeros((2 * PAD, CC), F32)
    for k in range(4):
        stacked = (centred[k] * row("merge_gain")[:, k * C : (k + 1) * C]).astype(BF)
        coarse = coarse + dot(stacked, vm["merge_weight"][k * C : (k + 1) * C])
    coarse = (coarse * scale).astype(BF).astype(F32)
    normed, scale = centre(coarse, row("coarse_gain"))
    packed = dot(normed, vm["coarse_qkv"][...]) * scale
    q = (packed[:, 0:CC] * Q_SCALE).astype(BF)
    k = packed[:, CC : 2 * CC].astype(BF)
    v = packed[:, 2 * CC : 3 * CC].astype(BF)
    heads = []
    for level in range(2):
        at = slice(level * PAD, (level + 1) * PAD)
        parts = []
        for j in range(3):
            cut = slice(j * 128, (j + 1) * 128)
            far = far_v[level, :, 0 : 4 * PAD]
            parts.append(attend4(q[at, cut], k[at, cut], v[at, cut], ones4[...], masks, far).astype(BF))
        heads.append(jnp.concatenate(parts, axis=1))
    heads = jnp.concatenate(heads, axis=0)
    coarse_out = (coarse + dot(heads, vm["coarse_proj"][...])).astype(BF)
    lifted = [dot(coarse_out, up_pad[:, k * 256 : k * 256 + C]) for k in range(4)]
    normed = [centre(x, row("up_gain")) for x in lifted]
    branch = dot(jnp.concatenate([n for n, _ in normed], axis=0), vm["out_weight"][...])
    encoded = [(group[k] + branch[k * 2 * PAD : (k + 1) * 2 * PAD] * normed[k][1]).astype(BF) for k in range(4)]
    three = []
    for level in range(2):
        order = range(4) if level == 0 else range(3, -1, -1)
        mine = jnp.concatenate([encoded[k][level * PAD : (level + 1) * PAD] for k in order], axis=0)
        quarters = dot(vm["send3"][...], mine).astype(BF)
        buf3[level, 0:PAD] = quarters[0:PAD]
        snd3[level] = quarters[PAD : 4 * PAD]
        three.append(send(2, level, (0, 1, 2), snd3, buf3, ENCODED))

    for level in range(2):
        for copy in three[level].values():
            copy.wait_recv()
        out_ref[level] = dot(vm["final"][level], buf3[level]).astype(BF)
    for copies in one + two + three:
        for copy in copies.values():
            copy.wait_send()


def body(lat_n, lon_n, tokens, norm_gain, qkv_weight, proj_weight, merge_gain, merge_weight, coarse_gain, *rest):
    coarse_qkv, coarse_proj, up_weight, up_gain, out_weight = rest
    table = tables()
    args = [
        tokens.reshape(2, OWN, C),
        norm_gain,
        qkv_weight,
        proj_weight,
        merge_gain,
        merge_weight,
        coarse_gain,
        coarse_qkv,
        coarse_proj,
        up_weight,
        up_gain,
        out_weight,
    ] + [jnp.asarray(table[n]) for n in TABLES]
    scratch = [pltpu.VMEM(a.shape, a.dtype) for a in args[1:]]
    scratch += [
        pltpu.VMEM((C, 768), BF),
        pltpu.VMEM((CC, 1024), BF),
        pltpu.VMEM((2, PAD, 6 * PAD), F32),
        pltpu.VMEM((2, OWN + HALO, C), BF),
        pltpu.VMEM((2, 4 * PAD + HALO2, C), BF),
        pltpu.VMEM((2, 4 * PAD, C), BF),
        pltpu.VMEM((2, HALO, C), BF),
        pltpu.VMEM((2, 3 * PAD, C), BF),
        pltpu.SemaphoreType.DMA((len(args) - 1,)),
        pltpu.SemaphoreType.DMA((2,)),
        pltpu.SemaphoreType.DMA((3, 2, 5)),
        pltpu.SemaphoreType.DMA((3, 2, 5)),
    ]
    out = pl.pallas_call(
        functools.partial(kernel, lat_n, lon_n),
        out_shape=jax.ShapeDtypeStruct((2, OWN, C), BF),
        in_specs=[pl.BlockSpec(memory_space=pltpu.HBM)] * len(args),
        out_specs=pl.BlockSpec(memory_space=pltpu.VMEM),
        scratch_shapes=scratch,
        compiler_params=pltpu.CompilerParams(
            collective_id=0, has_side_effects=True, vmem_limit_bytes=40 * 1024 * 1024
        ),
    )(*[pltpu.with_memory_space_constraint(a, pltpu.HBM) for a in args])
    return out.reshape(tokens.shape)


def solution(mesh):
    placed = (P(None, "lat", "lon", None),) + (P(),) * 11
    return jax.shard_map(
        functools.partial(body, mesh.shape["lat"], mesh.shape["lon"]),
        mesh=mesh,
        in_specs=placed,
        out_specs=P(None, "lat", "lon", None),
        check_vma=False,
    )
```

```python
import functools

import jax
import jax.numpy as jnp
import ml_dtypes
import numpy as np
from jax import lax
from jax.experimental import pallas as pl
from jax.experimental.pallas import tpu as pltpu
from jax.sharding import PartitionSpec as P

MESH = pl.DeviceIdType.MESH
BF = jnp.bfloat16
F32 = jnp.float32
EPSILON = 1e-05
C = 192
CC = 384
ROWS, COLS = 12, 24
OWN = ROWS * COLS
UNIT = 18
WIN = 72
PAD = 80
HEAD = 32
Q_SCALE = float(HEAD**-0.5 * np.log2(np.e))
V_SCALE = 2.0**-8
FAR = -1e30
HALO = 160
LAT_AT, LON_AT, DIAG_AT = 0, 64, 128
HALO2 = 208
MIRROR = (2, 3)
RESULTS = (
    (0, 4 * PAD, 32, 2),
    (16, 4 * PAD + 32, 32, 0),
    (32, 4 * PAD + 64, 32, 1),
    (PAD, 4 * PAD + 96, 48, 0),
    (2 * PAD, 4 * PAD + 144, 64, 1),
)
TOKENS = ((DIAG_AT, OWN + DIAG_AT, 32, 2), (LAT_AT, OWN + LAT_AT, 64, 0), (LON_AT, OWN + LON_AT, 64, 1))
ENCODED = ((2 * PAD, 3 * PAD, PAD, 2), (PAD, 2 * PAD, PAD, 0), (0, PAD, PAD, 1))


def one_hot(rows, cols, pairs):
    out = np.zeros((rows, cols), np.float32)
    for r, c in pairs:
        out[r, c] = 1.0
    return out.astype(ml_dtypes.bfloat16)


def halo_slot():
    for j in range(3):
        yield LAT_AT + j * UNIT, (0, j + 1)
        yield LON_AT + j * UNIT, (j + 1, 0)
    yield DIAG_AT, (0, 0)


def received(a, b):
    if a == 3 and b == 3:
        return DIAG_AT
    if a == 3:
        return LAT_AT + b * UNIT
    if b == 3:
        return LON_AT + a * UNIT
    return None


def window_row(a, b):
    return ((a // 2) * 2 + b // 2) * PAD + ((a % 2) * 2 + b % 2) * UNIT


def arrival(a, b):
    if a < 3 and b < 3:
        return window_row(a + 1, b + 1)
    which = {(3, 0): 1, (3, 1): 3, (3, 2): 3, (0, 3): 2, (1, 3): 4, (2, 3): 4, (3, 3): 0}[a, b]
    theirs = window_row(0 if a == 3 else a + 1, 0 if b == 3 else b + 1)
    return RESULTS[which][1] + theirs - RESULTS[which][0]


def natural(level, r, c):
    return (r if level == 0 else ROWS - 1 - r) * COLS + COLS - 1 - c


@functools.cache
def tables():
    units = [(a, b) for a in range(4) for b in range(4)]
    send1, gather1, final = [], [], []
    for level in range(2):

        def own(a, b, t, level=level):
            return natural(level, a * 3 + t // 6, b * 6 + t % 6)

        send1.append(
            one_hot(HALO, OWN, [(s + t, own(a, b, t)) for s, (a, b) in halo_slot() for t in range(UNIT)])
        )
        pairs = []
        for a, b in units:
            slot = received(a, b)
            for t in range(UNIT):
                source = own(a + 1, b + 1, t) if slot is None else OWN + slot + t
                pairs.append((window_row(a, b) + t, source))
        gather1.append(one_hot(4 * PAD, OWN + HALO, pairs))
        pairs = []
        for r in range(ROWS):
            for c in range(COLS):
                qr, qc = int(r < 6), int(c < 12)
                y, x = r % 6, c % 12
                k = y % 2 + 2 * (x % 2)
                t = (y // 2) * 6 + x // 2
                pairs.append((natural(level, r, c), (qr * 2 + qc) * PAD + k * UNIT + t))
        final.append(one_hot(OWN, 4 * PAD, pairs))
    pairs = []
    for y in range(ROWS):
        for x in range(COLS):
            a, b, t = y // 3, x // 6, (y % 3) * 6 + x % 6
            source = arrival(a, b) + t
            k = y % 2 + 2 * (x % 2)
            i, j = y // 2, x // 2
            cell = ((i // 3) * 2 + j // 6) * UNIT + (i % 3) * 6 + j % 6
            pairs.append((k * PAD + cell, source))
    gather2 = one_hot(4 * PAD, 4 * PAD + HALO2, pairs)
    pairs = []
    for quarter in range(4):
        for k in range(4):
            for t in range(UNIT):
                pairs.append((quarter * PAD + k * UNIT + t, k * PAD + quarter * UNIT + t))
    send3 = one_hot(4 * PAD, 4 * PAD, pairs)
    ones4 = np.zeros((4 * PAD, 128), np.float32)
    ones2 = np.zeros((224, 128), np.float32)
    for h in range(4):
        ones4[h * PAD : h * PAD + WIN, h * HEAD : (h + 1) * HEAD] = 1.0
    for h in range(2):
        ones2[64 + h * PAD : 64 + h * PAD + WIN, h * HEAD : (h + 1) * HEAD] = 1.0
    ones2[64 : 64 + WIN, 2 * HEAD :] = 1.0
    side_q = np.arange(PAD) >= WIN // 2
    side_k = np.arange(6 * PAD) % PAD >= WIN // 2
    far = np.where(side_q[:, None] != side_k[None, :], np.float32(FAR), np.float32(0.0))
    return dict(
        send1=np.stack(send1),
        gather1=np.stack(gather1),
        gather2=gather2,
        send3=send3,
        final=np.stack(final),
        ones4=ones4.astype(ml_dtypes.bfloat16),
        ones2=ones2.astype(ml_dtypes.bfloat16),
        far=far.astype(np.float32),
    )


ARGUMENTS = ("tokens", "norm_gain", "qkv_weight", "proj_weight", "merge_gain", "merge_weight", "coarse_gain", "coarse_qkv")
ARGUMENTS += ("coarse_proj", "up_weight", "up_gain", "out_weight")
EARLY = ("send1", "norm_gain", "qkv_weight", "far", "ones4", "ones2", "proj_weight", "gather1")
TABLES = ("send1", "gather1", "gather2", "send3", "final", "ones4", "ones2", "far")


def dot(a, b):
    return jnp.dot(a, b, preferred_element_type=F32)


def centre(values, gain):
    centred = values - jnp.mean(values, axis=-1, keepdims=True)
    spread = jnp.mean(centred * centred, axis=-1, keepdims=True)
    return (centred * gain).astype(BF), lax.rsqrt(spread + EPSILON)


def dot_t(a, b):
    return lax.dot_general(a, b, (((1,), (1,)), ((), ())), preferred_element_type=F32)


def shared(raised, values, ones):
    both = dot(raised, jnp.concatenate([values, ones], axis=1))
    return both[:, 0:128] / (both[:, 128:256] * V_SCALE)


def attend4(q, k, v, ones4, masks, far):
    keys = jnp.concatenate([k * m for m in masks], axis=0)
    raised = jnp.exp2(dot_t(q, keys) + far).astype(BF)
    small = v * jnp.bfloat16(V_SCALE)
    return shared(raised, jnp.concatenate([small * m for m in masks], axis=0), ones4)


def attend6(q, k, v, ones4, ones2, masks, far):
    zero = jnp.zeros((PAD, 128), BF)
    k0, k1 = k[:, 0:128], k[:, 128:256]
    keys = [jnp.concatenate([k0 * m, zero], axis=1) for m in masks]
    keys += [jnp.concatenate([zero, k1 * m], axis=1) for m in masks[0:2]]
    scores = dot_t(q, jnp.concatenate(keys, axis=0))
    if far is not None:
        scores = scores + far
    raised = jnp.exp2(scores).astype(BF)
    small = v * jnp.bfloat16(V_SCALE)
    v0, v1 = small[:, 0:128], small[:, 128:256]
    first = shared(raised[:, 0 : 4 * PAD], jnp.concatenate([v0 * m for m in masks], axis=0), ones4)
    last = [zero[0:64]] + [v1 * m for m in masks[0:2]]
    last = shared(raised[:, 256 : 6 * PAD], jnp.concatenate(last, axis=0), ones2)
    return jnp.concatenate([first, last], axis=1).astype(BF)


def kernel(lat_n, lon_n, *refs):
    names = list(ARGUMENTS)
    names += list(TABLES)
    hbm = dict(zip(names, refs))
    out_ref = refs[len(names)]
    scratch = refs[len(names) + 1 :]
    vm = dict(zip(names[1:], scratch))
    (qkv_pad, up_pad, far_v, buf1, buf2, buf3, snd1, snd3, load_sem, tok_sem, send_sem, recv_sem) = scratch[
        len(names) - 1 :
    ]

    lat, lon = lax.axis_index("lat"), lax.axis_index("lon")
    up, down = lax.rem(lat + 1, lat_n), lax.rem(lat + lat_n - 1, lat_n)
    east, west = lax.rem(lon + 1, lon_n), lax.rem(lon + lon_n - 1, lon_n)
    takers = (((down, lon), (lat, east), (down, east)), ((up, lon), (lat, east), (up, east)))
    owners = (((up, lon), (lat, west), (up, west)), ((down, lon), (lat, west), (down, west)))

    barrier = pltpu.get_barrier_semaphore()
    for device in ((up, lon), (down, lon), (lat, east), (lat, west)) + tuple((a, b) for a in (up, down) for b in (east, west)):
        pl.semaphore_signal(barrier, inc=1, device_id=device, device_id_type=MESH)

    loads = {}
    for level in range(2):
        loads["tokens", level] = pltpu.make_async_copy(
            hbm["tokens"].at[level], buf1.at[level, pl.ds(0, OWN)], tok_sem.at[level]
        )
        loads["tokens", level].start()
    order = ["send1"] + [n for n in EARLY if n != "send1"]
    order += [n for n in names[1:] if n not in order]

    def load(*wanted):
        for n in wanted:
            loads[n] = pltpu.make_async_copy(hbm[n], vm[n], load_sem.at[order.index(n)])
            loads[n].start()

    load("send1")

    def need(*wanted):
        for n in wanted:
            loads.pop(n).wait()

    def row(n):
        return vm[n][...].reshape(1, -1)

    def send(stage, level, which, source, target, plan):
        devices = (takers if stage < 2 else owners)[level]
        copies = {}
        for i in which:
            start, place, rows, neighbour = plan[i]
            copies[i] = pltpu.make_async_remote_copy(
                src_ref=source.at[level, pl.ds(start, rows)],
                dst_ref=target.at[level, pl.ds(place, rows)],
                send_sem=send_sem.at[stage, level, i],
                recv_sem=recv_sem.at[stage, level, i],
                device_id=devices[neighbour],
                device_id_type=MESH,
            )
            copies[i].start()
        return copies

    need("send1")
    for level in range(2):
        need(("tokens", level))
        snd1[level] = dot(vm["send1"][level], buf1[level, 0:OWN]).astype(BF)
    pl.semaphore_wait(barrier, 8)
    one = [send(0, level, (0, 1, 2), snd1, buf1, TOKENS) for level in range(2)]
    load(*order[1:])

    need("qkv_weight", "far")
    zero = jnp.zeros((C, 64), BF)
    for part in range(3):
        qkv_pad[:, part * 256 : part * 256 + C] = vm["qkv_weight"][:, part * C : (part + 1) * C]
        qkv_pad[:, part * 256 + C : (part + 1) * 256] = zero
    edge = (lat_n - 1, 0)
    for level in range(2):
        far_v[level] = jnp.where(lat == edge[level], vm["far"][...], 0.0)
    need("norm_gain", "ones4", "ones2", "proj_weight", "gather1")
    lane = lax.broadcasted_iota(jnp.int32, (PAD, 128), 1)
    masks = [jnp.where(lane // HEAD == h, 1.0, 0.0).astype(BF) for h in range(4)]
    ones4, ones2 = vm["ones4"], vm["ones2"]

    def fine(tokens, items):
        normed, scale = centre(tokens, row("norm_gain"))
        packed = dot(normed, qkv_pad[...]) * scale
        q = (packed[:, 0:256] * Q_SCALE).astype(BF)
        k = packed[:, 256:512].astype(BF)
        v = packed[:, 512:768].astype(BF)
        heads = []
        for i, (level, w) in enumerate(items):
            at = slice(i * PAD, (i + 1) * PAD)
            far = far_v[level] if w >= 2 else None
            heads.append(attend6(q[at], k[at], v[at], ones4[...], ones2[...], masks, far))
        heads = jnp.concatenate(heads, axis=0)[:, 0:C]
        result = (tokens + dot(heads, vm["proj_weight"][...])).astype(BF)
        for i, (level, w) in enumerate(items):
            buf2[level, w * PAD : (w + 1) * PAD] = result[i * PAD : (i + 1) * PAD]

    first = [dot(vm["gather1"][level, 0:PAD, 0:OWN], buf1[level, 0:OWN]) for level in range(2)]
    fine(jnp.concatenate(first, axis=0), [(0, 0), (1, 0)])

    two = [send(1, level, (0, 1, 2), buf2, buf2, RESULTS) for level in range(2)]

    near = OWN + LON_AT
    for level in range(2):
        one[level][1].wait_recv()
    rest = [dot(vm["gather1"][level, 2 * PAD : 3 * PAD, 0:near], buf1[level, 0:near]) for level in range(2)]
    fine(jnp.concatenate(rest, axis=0), [(0, 2), (1, 2)])
    for level in range(2):
        two[level].update(send(1, level, (4,), buf2, buf2, RESULTS))
    near = OWN + DIAG_AT
    for level in range(2):
        one[level][2].wait_recv()
    rest = [dot(vm["gather1"][level, PAD : 2 * PAD, 0:near], buf1[level, 0:near]) for level in range(2)]
    fine(jnp.concatenate(rest, axis=0), [(0, 1), (1, 1)])
    for level in range(2):
        two[level].update(send(1, level, (3,), buf2, buf2, RESULTS))
    for level in range(2):
        one[level][0].wait_recv()
    last = [dot(vm["gather1"][level, 3 * PAD : 4 * PAD], buf1[level]) for level in range(2)]
    fine(jnp.concatenate(last, axis=0), [(0, 3), (1, 3)])

    need("up_weight")
    for k in range(4):
        up_pad[:, k * 256 : k * 256 + C] = vm["up_weight"][:, k * C : (k + 1) * C]
    need("gather2", "send3", "merge_gain", "merge_weight", "coarse_gain", "coarse_qkv", "coarse_proj")
    need("up_gain", "out_weight", "final")

    for level in range(2):
        for copy in two[level].values():
            copy.wait_recv()
    cells = [dot(vm["gather2"][...], buf2[level]) for level in range(2)]
    group = [
        jnp.concatenate([cells[level][(k ^ m) * PAD : ((k ^ m) + 1) * PAD] for level, m in enumerate(MIRROR)], axis=0)
        for k in range(4)
    ]
    average = jnp.sum(group[0] + group[1] + group[2] + group[3], axis=-1, keepdims=True) * (1.0 / (4 * C))
    centred = [g - average for g in group]
    squares = [c * c for c in centred]
    spread = jnp.sum(squares[0] + squares[1] + squares[2] + squares[3], axis=-1, keepdims=True) * (1.0 / (4 * C))
    scale = lax.rsqrt(spread + EPSILON)
    coarse = jnp.zeros((2 * PAD, CC), F32)
    for k in range(4):
        stacked = (centred[k] * row("merge_gain")[:, k * C : (k + 1) * C]).astype(BF)
        coarse = coarse + dot(stacked, vm["merge_weight"][k * C : (k + 1) * C])
    coarse = (coarse * scale).astype(BF).astype(F32)
    normed, scale = centre(coarse, row("coarse_gain"))
    packed = dot(normed, vm["coarse_qkv"][...]) * scale
    q = (packed[:, 0:CC] * Q_SCALE).astype(BF)
    k = packed[:, CC : 2 * CC].astype(BF)
    v = packed[:, 2 * CC : 3 * CC].astype(BF)
    heads = []
    for level in range(2):
        at = slice(level * PAD, (level + 1) * PAD)
        parts = []
        for j in range(3):
            cut = slice(j * 128, (j + 1) * 128)
            far = far_v[level, :, 0 : 4 * PAD]
            parts.append(attend4(q[at, cut], k[at, cut], v[at, cut], ones4[...], masks, far).astype(BF))
        heads.append(jnp.concatenate(parts, axis=1))
    heads = jnp.concatenate(heads, axis=0)
    coarse_out = (coarse + dot(heads, vm["coarse_proj"][...])).astype(BF)
    lifted = [dot(coarse_out, up_pad[:, k * 256 : k * 256 + C]) for k in range(4)]
    normed = [centre(x, row("up_gain")) for x in lifted]
    branch = dot(jnp.concatenate([n for n, _ in normed], axis=0), vm["out_weight"][...])
    encoded = [(group[k] + branch[k * 2 * PAD : (k + 1) * 2 * PAD] * normed[k][1]).astype(BF) for k in range(4)]
    three = []
    for level in range(2):
        mine = [encoded[k ^ MIRROR[level]][level * PAD : (level + 1) * PAD] for k in range(4)]
        mine = jnp.concatenate(mine, axis=0)
        quarters = dot(vm["send3"][...], mine).astype(BF)
        buf3[level, 0:PAD] = quarters[0:PAD]
        snd3[level] = quarters[PAD : 4 * PAD]
        three.append(send(2, level, (0, 1, 2), snd3, buf3, ENCODED))

    for level in range(2):
        for copy in three[level].values():
            copy.wait_recv()
        out_ref[level] = dot(vm["final"][level], buf3[level]).astype(BF)
    for copies in one + two + three:
        for copy in copies.values():
            copy.wait_send()


def body(lat_n, lon_n, tokens, norm_gain, qkv_weight, proj_weight, merge_gain, merge_weight, coarse_gain, *rest):
    coarse_qkv, coarse_proj, up_weight, up_gain, out_weight = rest
    table = tables()
    args = [
        tokens.reshape(2, OWN, C),
        norm_gain,
        qkv_weight,
        proj_weight,
        merge_gain,
        merge_weight,
        coarse_gain,
        coarse_qkv,
        coarse_proj,
        up_weight,
        up_gain,
        out_weight,
    ] + [jnp.asarray(table[n]) for n in TABLES]
    scratch = [pltpu.VMEM(a.shape, a.dtype) for a in args[1:]]
    scratch += [
        pltpu.VMEM((C, 768), BF),
        pltpu.VMEM((CC, 1024), BF),
        pltpu.VMEM((2, PAD, 6 * PAD), F32),
        pltpu.VMEM((2, OWN + HALO, C), BF),
        pltpu.VMEM((2, 4 * PAD + HALO2, C), BF),
        pltpu.VMEM((2, 4 * PAD, C), BF),
        pltpu.VMEM((2, HALO, C), BF),
        pltpu.VMEM((2, 3 * PAD, C), BF),
        pltpu.SemaphoreType.DMA((len(args) - 1,)),
        pltpu.SemaphoreType.DMA((2,)),
        pltpu.SemaphoreType.DMA((3, 2, 5)),
        pltpu.SemaphoreType.DMA((3, 2, 5)),
    ]
    out = pl.pallas_call(
        functools.partial(kernel, lat_n, lon_n),
        out_shape=jax.ShapeDtypeStruct((2, OWN, C), BF),
        in_specs=[pl.BlockSpec(memory_space=pltpu.HBM)] * len(args),
        out_specs=pl.BlockSpec(memory_space=pltpu.VMEM),
        scratch_shapes=scratch,
        compiler_params=pltpu.CompilerParams(
            collective_id=0, has_side_effects=True, vmem_limit_bytes=40 * 1024 * 1024
        ),
    )(*[pltpu.with_memory_space_constraint(a, pltpu.HBM) for a in args])
    return out.reshape(tokens.shape)


def solution(mesh):
    placed = (P(None, "lat", "lon", None),) + (P(),) * 11
    return jax.shard_map(
        functools.partial(body, mesh.shape["lat"], mesh.shape["lon"]),
        mesh=mesh,
        in_specs=placed,
        out_specs=P(None, "lat", "lon", None),
        check_vma=False,
    )
```

```python
import functools

import jax
import jax.numpy as jnp
import ml_dtypes
import numpy as np
from jax import lax
from jax.experimental import pallas as pl
from jax.experimental.pallas import tpu as pltpu
from jax.sharding import PartitionSpec as P

MESH = pl.DeviceIdType.MESH
BF = jnp.bfloat16
F32 = jnp.float32
EPSILON = 1e-05
C = 192
CC = 384
ROWS, COLS = 12, 24
OWN = ROWS * COLS
UNIT = 18
WIN = 72
PAD = 80
HEAD = 32
Q_SCALE = float(HEAD**-0.5 * np.log2(np.e))
V_SCALE = 2.0**-8
FAR = -1e30
HALO = 160
LAT_AT, LON_AT, DIAG_AT = 0, 64, 128
HALO2 = 192
MIRROR = (2, 3)
RESULTS = (
    (0, 4 * PAD, 32, 2),
    (16, 4 * PAD + 32, 32, 0),
    (32, 4 * PAD + 64, 32, 1),
    (PAD, 4 * PAD + 96, 48, 0),
    (2 * PAD, 4 * PAD + 144, 48, 1),
)
TOKENS = ((LON_AT, OWN + LON_AT, 64, 1), (LAT_AT, OWN + LAT_AT, 64, 0), (DIAG_AT, OWN + DIAG_AT, 32, 2))
ENCODED = ((2 * PAD, 3 * PAD, PAD, 2), (PAD, 2 * PAD, PAD, 0), (0, PAD, PAD, 1))


def one_hot(rows, cols, pairs):
    out = np.zeros((rows, cols), np.float32)
    for r, c in pairs:
        out[r, c] = 1.0
    return out.astype(ml_dtypes.bfloat16)


def halo_slot():
    for j in range(3):
        yield LAT_AT + j * UNIT, (0, j + 1)
        yield LON_AT + j * UNIT, (j + 1, 0)
    yield DIAG_AT, (0, 0)


def received(a, b):
    if a == 3 and b == 3:
        return DIAG_AT
    if a == 3:
        return LAT_AT + b * UNIT
    if b == 3:
        return LON_AT + a * UNIT
    return None


def window_row(a, b):
    window, inner = (a // 2) * 2 + b // 2, (a % 2) * 2 + b % 2
    if window == 2:
        inner = (b % 2) * 2 + a % 2
    return window * PAD + inner * UNIT


def arrival(a, b):
    if a < 3 and b < 3:
        return window_row(a + 1, b + 1)
    which = {(3, 0): 1, (3, 1): 3, (3, 2): 3, (0, 3): 2, (1, 3): 4, (2, 3): 4, (3, 3): 0}[a, b]
    theirs = window_row(0 if a == 3 else a + 1, 0 if b == 3 else b + 1)
    return RESULTS[which][1] + theirs - RESULTS[which][0]


def natural(level, r, c):
    return (r if level == 0 else ROWS - 1 - r) * COLS + COLS - 1 - c


@functools.cache
def tables():
    units = [(a, b) for a in range(4) for b in range(4)]
    send1, gather1, final = [], [], []
    for level in range(2):

        def own(a, b, t, level=level):
            return natural(level, a * 3 + t // 6, b * 6 + t % 6)

        send1.append(
            one_hot(HALO, OWN, [(s + t, own(a, b, t)) for s, (a, b) in halo_slot() for t in range(UNIT)])
        )
        pairs = []
        for a, b in units:
            slot = received(a, b)
            for t in range(UNIT):
                source = own(a + 1, b + 1, t) if slot is None else OWN + slot + t
                pairs.append((window_row(a, b) + t, source))
        gather1.append(one_hot(4 * PAD, OWN + HALO, pairs))
        pairs = []
        for r in range(ROWS):
            for c in range(COLS):
                qr, qc = int(r < 6), int(c < 12)
                y, x = r % 6, c % 12
                k = y % 2 + 2 * (x % 2)
                t = (y // 2) * 6 + x // 2
                pairs.append((natural(level, r, c), (qr * 2 + qc) * PAD + k * UNIT + t))
        final.append(one_hot(OWN, 4 * PAD, pairs))
    pairs = []
    for y in range(ROWS):
        for x in range(COLS):
            a, b, t = y // 3, x // 6, (y % 3) * 6 + x % 6
            source = arrival(a, b) + t
            k = y % 2 + 2 * (x % 2)
            i, j = y // 2, x // 2
            cell = ((i // 3) * 2 + j // 6) * UNIT + (i % 3) * 6 + j % 6
            pairs.append((k * PAD + cell, source))
    gather2 = one_hot(4 * PAD, 4 * PAD + HALO2, pairs)
    pairs = []
    for quarter in range(4):
        for k in range(4):
            for t in range(UNIT):
                pairs.append((quarter * PAD + k * UNIT + t, k * PAD + quarter * UNIT + t))
    send3 = one_hot(4 * PAD, 4 * PAD, pairs)
    ones4 = np.zeros((4 * PAD, 128), np.float32)
    ones2 = np.zeros((224, 128), np.float32)
    for h in range(4):
        ones4[h * PAD : h * PAD + WIN, h * HEAD : (h + 1) * HEAD] = 1.0
    for h in range(2):
        ones2[64 + h * PAD : 64 + h * PAD + WIN, h * HEAD : (h + 1) * HEAD] = 1.0
    ones2[64 : 64 + WIN, 2 * HEAD :] = 1.0
    far = []
    for by_column in (False, True):
        units_of = np.arange(PAD) // UNIT
        side = (units_of % 2 if by_column else units_of // 2) == 1
        far.append(np.where(side[:, None] != np.tile(side, 6)[None, :], np.float32(FAR), np.float32(0.0)))
    far = np.stack(far)
    return dict(
        send1=np.stack(send1),
        gather1=np.stack(gather1),
        gather2=gather2,
        send3=send3,
        final=np.stack(final),
        ones4=ones4.astype(ml_dtypes.bfloat16),
        ones2=ones2.astype(ml_dtypes.bfloat16),
        far=far.astype(ml_dtypes.bfloat16),
    )


ARGUMENTS = ("tokens", "norm_gain", "qkv_weight", "proj_weight", "merge_gain", "merge_weight", "coarse_gain", "coarse_qkv")
ARGUMENTS += ("coarse_proj", "up_weight", "up_gain", "out_weight")
EARLY = ("send1", "norm_gain", "qkv_weight", "far", "ones4", "ones2", "proj_weight", "gather1")
TABLES = ("send1", "gather1", "gather2", "send3", "final", "ones4", "ones2", "far")


def dot(a, b):
    return jnp.dot(a, b, preferred_element_type=F32)


def centre(values, gain):
    centred = values - jnp.mean(values, axis=-1, keepdims=True)
    spread = jnp.mean(centred * centred, axis=-1, keepdims=True)
    return (centred * gain).astype(BF), lax.rsqrt(spread + EPSILON)


def dot_t(a, b):
    return lax.dot_general(a, b, (((1,), (1,)), ((), ())), preferred_element_type=F32)


def shared(raised, values, ones):
    both = dot(raised, jnp.concatenate([values, ones], axis=1))
    return both[:, 0:128] / (both[:, 128:256] * V_SCALE)


def attend4(q, k, v, ones4, masks, far):
    keys = jnp.concatenate([k * m for m in masks], axis=0)
    raised = jnp.exp2(dot_t(q, keys) + far).astype(BF)
    small = v * jnp.bfloat16(V_SCALE)
    return shared(raised, jnp.concatenate([small * m for m in masks], axis=0), ones4)


def attend6(q, k, v, ones4, ones2, masks, far):
    zero = jnp.zeros((PAD, 128), BF)
    k0, k1 = k[:, 0:128], k[:, 128:256]
    keys = [jnp.concatenate([k0 * m, zero], axis=1) for m in masks]
    keys += [jnp.concatenate([zero, k1 * m], axis=1) for m in masks[0:2]]
    scores = dot_t(q, jnp.concatenate(keys, axis=0))
    if far is not None:
        scores = scores + far
    raised = jnp.exp2(scores).astype(BF)
    small = v * jnp.bfloat16(V_SCALE)
    v0, v1 = small[:, 0:128], small[:, 128:256]
    first = shared(raised[:, 0 : 4 * PAD], jnp.concatenate([v0 * m for m in masks], axis=0), ones4)
    last = [zero[0:64]] + [v1 * m for m in masks[0:2]]
    last = shared(raised[:, 256 : 6 * PAD], jnp.concatenate(last, axis=0), ones2)
    return jnp.concatenate([first, last], axis=1).astype(BF)


def kernel(lat_n, lon_n, *refs):
    names = list(ARGUMENTS)
    names += list(TABLES)
    hbm = dict(zip(names, refs))
    out_ref = refs[len(names)]
    scratch = refs[len(names) + 1 :]
    vm = dict(zip(names[1:], scratch))
    (qkv_pad, up_pad, far_v, buf1, buf2, buf3, snd1, snd3, load_sem, tok_sem, send_sem, recv_sem) = scratch[
        len(names) - 1 :
    ]

    lat, lon = lax.axis_index("lat"), lax.axis_index("lon")
    up, down = lax.rem(lat + 1, lat_n), lax.rem(lat + lat_n - 1, lat_n)
    east, west = lax.rem(lon + 1, lon_n), lax.rem(lon + lon_n - 1, lon_n)
    takers = (((down, lon), (lat, east), (down, east)), ((up, lon), (lat, east), (up, east)))
    owners = (((up, lon), (lat, west), (up, west)), ((down, lon), (lat, west), (down, west)))

    barrier = pltpu.get_barrier_semaphore()
    for device in ((up, lon), (down, lon), (lat, east), (lat, west)) + tuple((a, b) for a in (up, down) for b in (east, west)):
        pl.semaphore_signal(barrier, inc=1, device_id=device, device_id_type=MESH)

    loads = {}
    for level in range(2):
        loads["tokens", level] = pltpu.make_async_copy(
            hbm["tokens"].at[level], buf1.at[level, pl.ds(0, OWN)], tok_sem.at[level]
        )
        loads["tokens", level].start()
    order = ["send1"] + [n for n in EARLY if n != "send1"]
    order += [n for n in names[1:] if n not in order]

    def load(*wanted):
        for n in wanted:
            loads[n] = pltpu.make_async_copy(hbm[n], vm[n], load_sem.at[order.index(n)])
            loads[n].start()

    load(*order[:len(EARLY)])

    def need(*wanted):
        for n in wanted:
            loads.pop(n).wait()

    def row(n):
        return vm[n][...].reshape(1, -1)

    def send(stage, level, which, source, target, plan):
        devices = (takers if stage < 2 else owners)[level]
        copies = {}
        for i in which:
            start, place, rows, neighbour = plan[i]
            copies[i] = pltpu.make_async_remote_copy(
                src_ref=source.at[level, pl.ds(start, rows)],
                dst_ref=target.at[level, pl.ds(place, rows)],
                send_sem=send_sem.at[stage, level, i],
                recv_sem=recv_sem.at[stage, level, i],
                device_id=devices[neighbour],
                device_id_type=MESH,
            )
            copies[i].start()
        return copies

    need("send1")
    for level in range(2):
        need(("tokens", level))
        snd1[level] = dot(vm["send1"][level], buf1[level, 0:OWN]).astype(BF)
    pl.semaphore_wait(barrier, 8)
    one = [{}, {}]
    for i in range(3):
        for level in range(2):
            one[level].update(send(0, level, (i,), snd1, buf1, TOKENS))
    load(*order[len(EARLY):])

    need("qkv_weight", "far")
    zero = jnp.zeros((C, 64), BF)
    for part in range(3):
        qkv_pad[:, part * 256 : part * 256 + C] = vm["qkv_weight"][:, part * C : (part + 1) * C]
        qkv_pad[:, part * 256 + C : (part + 1) * 256] = zero
    edge = (lat_n - 1, 0)
    for level in range(2):
        far_v[level] = jnp.where(lat == edge[level], vm["far"][...].astype(F32), 0.0)
    need("norm_gain", "ones4", "ones2", "proj_weight", "gather1")
    lane = lax.broadcasted_iota(jnp.int32, (PAD, 128), 1)
    masks = [jnp.where(lane // HEAD == h, 1.0, 0.0).astype(BF) for h in range(4)]
    ones4, ones2 = vm["ones4"], vm["ones2"]

    def fine(tokens, items):
        normed, scale = centre(tokens, row("norm_gain"))
        packed = dot(normed, qkv_pad[...]) * scale
        q = (packed[:, 0:256] * Q_SCALE).astype(BF)
        k = packed[:, 256:512].astype(BF)
        v = packed[:, 512:768].astype(BF)
        heads = []
        for i, (level, w) in enumerate(items):
            at = slice(i * PAD, (i + 1) * PAD)
            far = far_v[level, 3 - w] if w >= 2 else None
            heads.append(attend6(q[at], k[at], v[at], ones4[...], ones2[...], masks, far))
        heads = jnp.concatenate(heads, axis=0)[:, 0:C]
        result = (tokens + dot(heads, vm["proj_weight"][...])).astype(BF)
        for i, (level, w) in enumerate(items):
            buf2[level, w * PAD : (w + 1) * PAD] = result[i * PAD : (i + 1) * PAD]

    first = [dot(vm["gather1"][level, 0:PAD, 0:OWN], buf1[level, 0:OWN]) for level in range(2)]
    fine(jnp.concatenate(first, axis=0), [(0, 0), (1, 0)])

    two = [send(1, level, (0, 1, 2), buf2, buf2, RESULTS) for level in range(2)]

    near = OWN + LON_AT
    for level in range(2):
        one[level][1].wait_recv()
    rest = [dot(vm["gather1"][level, 2 * PAD : 3 * PAD, 0:near], buf1[level, 0:near]) for level in range(2)]
    fine(jnp.concatenate(rest, axis=0), [(0, 2), (1, 2)])
    for level in range(2):
        two[level].update(send(1, level, (4,), buf2, buf2, RESULTS))
    near = OWN + DIAG_AT
    for level in range(2):
        one[level][0].wait_recv()
    rest = [dot(vm["gather1"][level, PAD : 2 * PAD, 0:near], buf1[level, 0:near]) for level in range(2)]
    fine(jnp.concatenate(rest, axis=0), [(0, 1), (1, 1)])
    for level in range(2):
        two[level].update(send(1, level, (3,), buf2, buf2, RESULTS))
    for level in range(2):
        one[level][2].wait_recv()
    last = [dot(vm["gather1"][level, 3 * PAD : 4 * PAD], buf1[level]) for level in range(2)]
    fine(jnp.concatenate(last, axis=0), [(0, 3), (1, 3)])

    need("up_weight")
    for k in range(4):
        up_pad[:, k * 256 : k * 256 + C] = vm["up_weight"][:, k * C : (k + 1) * C]
    need("gather2", "send3", "merge_gain", "merge_weight", "coarse_gain", "coarse_qkv", "coarse_proj")
    need("up_gain", "out_weight", "final")

    for level in range(2):
        for copy in two[level].values():
            copy.wait_recv()
    cells = [dot(vm["gather2"][...], buf2[level]) for level in range(2)]
    group = [
        jnp.concatenate([cells[level][(k ^ m) * PAD : ((k ^ m) + 1) * PAD] for level, m in enumerate(MIRROR)], axis=0)
        for k in range(4)
    ]
    average = jnp.sum(group[0] + group[1] + group[2] + group[3], axis=-1, keepdims=True) * (1.0 / (4 * C))
    centred = [g - average for g in group]
    squares = [c * c for c in centred]
    spread = jnp.sum(squares[0] + squares[1] + squares[2] + squares[3], axis=-1, keepdims=True) * (1.0 / (4 * C))
    scale = lax.rsqrt(spread + EPSILON)
    coarse = jnp.zeros((2 * PAD, CC), F32)
    for k in range(4):
        stacked = (centred[k] * row("merge_gain")[:, k * C : (k + 1) * C]).astype(BF)
        coarse = coarse + dot(stacked, vm["merge_weight"][k * C : (k + 1) * C])
    coarse = (coarse * scale).astype(BF).astype(F32)
    normed, scale = centre(coarse, row("coarse_gain"))
    packed = dot(normed, vm["coarse_qkv"][...]) * scale
    q = (packed[:, 0:CC] * Q_SCALE).astype(BF)
    k = packed[:, CC : 2 * CC].astype(BF)
    v = packed[:, 2 * CC : 3 * CC].astype(BF)
    heads = []
    for level in range(2):
        at = slice(level * PAD, (level + 1) * PAD)
        parts = []
        for j in range(3):
            cut = slice(j * 128, (j + 1) * 128)
            far = far_v[level, 0, :, 0 : 4 * PAD]
            parts.append(attend4(q[at, cut], k[at, cut], v[at, cut], ones4[...], masks, far).astype(BF))
        heads.append(jnp.concatenate(parts, axis=1))
    heads = jnp.concatenate(heads, axis=0)
    coarse_out = (coarse + dot(heads, vm["coarse_proj"][...])).astype(BF)
    lifted = [dot(coarse_out, up_pad[:, k * 256 : k * 256 + C]) for k in range(4)]
    normed = [centre(x, row("up_gain")) for x in lifted]
    branch = dot(jnp.concatenate([n for n, _ in normed], axis=0), vm["out_weight"][...])
    encoded = [(group[k] + branch[k * 2 * PAD : (k + 1) * 2 * PAD] * normed[k][1]).astype(BF) for k in range(4)]
    three = []
    for level in range(2):
        mine = [encoded[k ^ MIRROR[level]][level * PAD : (level + 1) * PAD] for k in range(4)]
        mine = jnp.concatenate(mine, axis=0)
        quarters = dot(vm["send3"][...], mine).astype(BF)
        buf3[level, 0:PAD] = quarters[0:PAD]
        snd3[level] = quarters[PAD : 4 * PAD]
        three.append(send(2, level, (0, 1, 2), snd3, buf3, ENCODED))

    for level in range(2):
        for copy in three[level].values():
            copy.wait_recv()
        out_ref[level] = dot(vm["final"][level], buf3[level]).astype(BF)
    for copies in one + two + three:
        for copy in copies.values():
            copy.wait_send()


def body(lat_n, lon_n, tokens, norm_gain, qkv_weight, proj_weight, merge_gain, merge_weight, coarse_gain, *rest):
    coarse_qkv, coarse_proj, up_weight, up_gain, out_weight = rest
    table = tables()
    args = [
        tokens.reshape(2, OWN, C),
        norm_gain,
        qkv_weight,
        proj_weight,
        merge_gain,
        merge_weight,
        coarse_gain,
        coarse_qkv,
        coarse_proj,
        up_weight,
        up_gain,
        out_weight,
    ] + [jnp.asarray(table[n]) for n in TABLES]
    scratch = [pltpu.VMEM(a.shape, a.dtype) for a in args[1:]]
    scratch += [
        pltpu.VMEM((C, 768), BF),
        pltpu.VMEM((CC, 1024), BF),
        pltpu.VMEM((2, 2, PAD, 6 * PAD), F32),
        pltpu.VMEM((2, OWN + HALO, C), BF),
        pltpu.VMEM((2, 4 * PAD + HALO2, C), BF),
        pltpu.VMEM((2, 4 * PAD, C), BF),
        pltpu.VMEM((2, HALO, C), BF),
        pltpu.VMEM((2, 3 * PAD, C), BF),
        pltpu.SemaphoreType.DMA((len(args) - 1,)),
        pltpu.SemaphoreType.DMA((2,)),
        pltpu.SemaphoreType.DMA((3, 2, 5)),
        pltpu.SemaphoreType.DMA((3, 2, 5)),
    ]
    out = pl.pallas_call(
        functools.partial(kernel, lat_n, lon_n),
        out_shape=jax.ShapeDtypeStruct((2, OWN, C), BF),
        in_specs=[pl.BlockSpec(memory_space=pltpu.HBM)] * len(args),
        out_specs=pl.BlockSpec(memory_space=pltpu.VMEM),
        scratch_shapes=scratch,
        compiler_params=pltpu.CompilerParams(
            collective_id=0, has_side_effects=True, vmem_limit_bytes=40 * 1024 * 1024
        ),
    )(*[pltpu.with_memory_space_constraint(a, pltpu.HBM) for a in args])
    return out.reshape(tokens.shape)


def solution(mesh):
    placed = (P(None, "lat", "lon", None),) + (P(),) * 11
    return jax.shard_map(
        functools.partial(body, mesh.shape["lat"], mesh.shape["lon"]),
        mesh=mesh,
        in_specs=placed,
        out_specs=P(None, "lat", "lon", None),
        check_vma=False,
    )
```

```python
import functools

import jax
import jax.numpy as jnp
import ml_dtypes
import numpy as np
from jax import lax
from jax.experimental import pallas as pl
from jax.experimental.pallas import tpu as pltpu
from jax.sharding import PartitionSpec as P

MESH = pl.DeviceIdType.MESH
BF = jnp.bfloat16
F32 = jnp.float32
EPSILON = 1e-05
C = 192
CC = 384
ROWS, COLS = 12, 24
OWN = ROWS * COLS
UNIT = 18
WIN = 72
PAD = 80
HEAD = 32
Q_SCALE = float(HEAD**-0.5 * np.log2(np.e))
V_SCALE = 2.0**-8
FAR = -1e30
HALO = 160
LAT_AT, LON_AT, DIAG_AT = 0, 64, 128
HALO2 = 192
MIRROR = (2, 3)
RESULTS = (
    (0, 4 * PAD, 32, 2),
    (16, 4 * PAD + 32, 32, 0),
    (32, 4 * PAD + 64, 32, 1),
    (PAD, 4 * PAD + 96, 48, 0),
    (2 * PAD, 4 * PAD + 144, 48, 1),
)
TOKENS = ((LON_AT, OWN + LON_AT, 64, 1), (LAT_AT, OWN + LAT_AT, 64, 0), (DIAG_AT, OWN + DIAG_AT, 32, 2))
ENCODED = ((2 * PAD, 3 * PAD, PAD, 2), (PAD, 2 * PAD, PAD, 0), (0, PAD, PAD, 1))


def one_hot(rows, cols, pairs):
    out = np.zeros((rows, cols), np.float32)
    for r, c in pairs:
        out[r, c] = 1.0
    return out.astype(ml_dtypes.bfloat16)


def halo_slot():
    for j in range(3):
        yield LAT_AT + j * UNIT, (0, j + 1)
        yield LON_AT + j * UNIT, (j + 1, 0)
    yield DIAG_AT, (0, 0)


def received(a, b):
    if a == 3 and b == 3:
        return DIAG_AT
    if a == 3:
        return LAT_AT + b * UNIT
    if b == 3:
        return LON_AT + a * UNIT
    return None


def window_row(a, b):
    window, inner = (a // 2) * 2 + b // 2, (a % 2) * 2 + b % 2
    if window == 2:
        inner = (b % 2) * 2 + a % 2
    return window * PAD + inner * UNIT


def arrival(a, b):
    if a < 3 and b < 3:
        return window_row(a + 1, b + 1)
    which = {(3, 0): 1, (3, 1): 3, (3, 2): 3, (0, 3): 2, (1, 3): 4, (2, 3): 4, (3, 3): 0}[a, b]
    theirs = window_row(0 if a == 3 else a + 1, 0 if b == 3 else b + 1)
    return RESULTS[which][1] + theirs - RESULTS[which][0]


def natural(level, r, c):
    return (r if level == 0 else ROWS - 1 - r) * COLS + COLS - 1 - c


@functools.cache
def tables():
    units = [(a, b) for a in range(4) for b in range(4)]
    send1, gather1, final = [], [], []
    for level in range(2):

        def own(a, b, t, level=level):
            return natural(level, a * 3 + t // 6, b * 6 + t % 6)

        send1.append(
            one_hot(HALO, OWN, [(s + t, own(a, b, t)) for s, (a, b) in halo_slot() for t in range(UNIT)])
        )
        pairs = []
        for a, b in units:
            slot = received(a, b)
            for t in range(UNIT):
                source = own(a + 1, b + 1, t) if slot is None else OWN + slot + t
                pairs.append((window_row(a, b) + t, source))
        gather1.append(one_hot(4 * PAD, OWN + HALO, pairs))
        pairs = []
        for r in range(ROWS):
            for c in range(COLS):
                qr, qc = int(r < 6), int(c < 12)
                y, x = r % 6, c % 12
                k = y % 2 + 2 * (x % 2)
                t = (y // 2) * 6 + x // 2
                pairs.append((natural(level, r, c), (qr * 2 + qc) * PAD + k * UNIT + t))
        final.append(one_hot(OWN, 4 * PAD, pairs))
    pairs = []
    for y in range(ROWS):
        for x in range(COLS):
            a, b, t = y // 3, x // 6, (y % 3) * 6 + x % 6
            source = arrival(a, b) + t
            k = y % 2 + 2 * (x % 2)
            i, j = y // 2, x // 2
            cell = ((i // 3) * 2 + j // 6) * UNIT + (i % 3) * 6 + j % 6
            pairs.append((k * PAD + cell, source))
    gather2 = one_hot(4 * PAD, 4 * PAD + HALO2, pairs)
    pairs = []
    for quarter in range(4):
        for k in range(4):
            for t in range(UNIT):
                pairs.append((quarter * PAD + k * UNIT + t, k * PAD + quarter * UNIT + t))
    send3 = one_hot(4 * PAD, 4 * PAD, pairs)
    ones4 = np.zeros((4 * PAD, 128), np.float32)
    ones2 = np.zeros((224, 128), np.float32)
    for h in range(4):
        ones4[h * PAD : h * PAD + WIN, h * HEAD : (h + 1) * HEAD] = 1.0
    for h in range(2):
        ones2[64 + h * PAD : 64 + h * PAD + WIN, h * HEAD : (h + 1) * HEAD] = 1.0
    ones2[64 : 64 + WIN, 2 * HEAD :] = 1.0
    far = []
    for by_column in (False, True):
        units_of = np.arange(PAD) // UNIT
        side = (units_of % 2 if by_column else units_of // 2) == 1
        far.append(np.where(side[:, None] != np.tile(side, 6)[None, :], np.float32(FAR), np.float32(0.0)))
    far = np.stack(far)
    return dict(
        send1=np.stack(send1),
        gather1=np.stack(gather1),
        gather2=gather2,
        send3=send3,
        final=np.stack(final),
        ones4=ones4.astype(ml_dtypes.bfloat16),
        ones2=ones2.astype(ml_dtypes.bfloat16),
        far=far.astype(ml_dtypes.bfloat16),
    )


ARGUMENTS = ("tokens", "norm_gain", "qkv_weight", "proj_weight", "merge_gain", "merge_weight", "coarse_gain", "coarse_qkv")
ARGUMENTS += ("coarse_proj", "up_weight", "up_gain", "out_weight")
EARLY = ("send1", "norm_gain", "qkv_weight", "far", "ones4", "ones2", "proj_weight", "gather1")
TABLES = ("send1", "gather1", "gather2", "send3", "final", "ones4", "ones2", "far")


def dot(a, b):
    return jnp.dot(a, b, preferred_element_type=F32)


def centre(values, gain):
    centred = values - jnp.mean(values, axis=-1, keepdims=True)
    spread = jnp.mean(centred * centred, axis=-1, keepdims=True)
    return (centred * gain).astype(BF), lax.rsqrt(spread + EPSILON)


def dot_t(a, b):
    return lax.dot_general(a, b, (((1,), (1,)), ((), ())), preferred_element_type=F32)


def shared(raised, values, ones):
    both = dot(raised, jnp.concatenate([values, ones], axis=1))
    return both[:, 0:128] / (both[:, 128:256] * V_SCALE)


def attend4(q, k, v, ones4, masks, far):
    keys = jnp.concatenate([k * m for m in masks], axis=0)
    raised = jnp.exp2(dot_t(q, keys) + far).astype(BF)
    small = v * jnp.bfloat16(V_SCALE)
    return shared(raised, jnp.concatenate([small * m for m in masks], axis=0), ones4)


def attend6(q, k, v, ones4, ones2, masks, far):
    zero = jnp.zeros((PAD, 128), BF)
    k0, k1 = k[:, 0:128], k[:, 128:256]
    keys = [jnp.concatenate([k0 * m, zero], axis=1) for m in masks]
    keys += [jnp.concatenate([zero, k1 * m], axis=1) for m in masks[0:2]]
    scores = dot_t(q, jnp.concatenate(keys, axis=0))
    if far is not None:
        scores = scores + far
    raised = jnp.exp2(scores).astype(BF)
    small = v * jnp.bfloat16(V_SCALE)
    v0, v1 = small[:, 0:128], small[:, 128:256]
    first = shared(raised[:, 0 : 4 * PAD], jnp.concatenate([v0 * m for m in masks], axis=0), ones4)
    last = [zero[0:64]] + [v1 * m for m in masks[0:2]]
    last = shared(raised[:, 256 : 6 * PAD], jnp.concatenate(last, axis=0), ones2)
    return jnp.concatenate([first, last], axis=1).astype(BF)


def kernel(lat_n, lon_n, *refs):
    names = list(ARGUMENTS)
    names += list(TABLES)
    hbm = dict(zip(names, refs))
    out_ref = refs[len(names)]
    scratch = refs[len(names) + 1 :]
    vm = dict(zip(names[1:], scratch))
    (qkv_pad, up_pad, far_v, buf1, buf2, buf3, snd1, snd3, load_sem, tok_sem, send_sem, recv_sem) = scratch[
        len(names) - 1 :
    ]

    lat, lon = lax.axis_index("lat"), lax.axis_index("lon")
    up, down = lax.rem(lat + 1, lat_n), lax.rem(lat + lat_n - 1, lat_n)
    east, west = lax.rem(lon + 1, lon_n), lax.rem(lon + lon_n - 1, lon_n)
    takers = (((down, lon), (lat, east), (down, east)), ((up, lon), (lat, east), (up, east)))
    owners = (((up, lon), (lat, west), (up, west)), ((down, lon), (lat, west), (down, west)))

    barrier = pltpu.get_barrier_semaphore()
    for device in ((up, lon), (down, lon), (lat, east), (lat, west)) + tuple((a, b) for a in (up, down) for b in (east, west)):
        pl.semaphore_signal(barrier, inc=1, device_id=device, device_id_type=MESH)

    loads = {}
    for level in range(2):
        loads["tokens", level] = pltpu.make_async_copy(
            hbm["tokens"].at[level], buf1.at[level, pl.ds(0, OWN)], tok_sem.at[level]
        )
        loads["tokens", level].start()
    order = ["send1"] + [n for n in EARLY if n != "send1"]
    order += [n for n in names[1:] if n not in order]

    def load(*wanted):
        for n in wanted:
            loads[n] = pltpu.make_async_copy(hbm[n], vm[n], load_sem.at[order.index(n)])
            loads[n].start()

    load(*order[:len(EARLY)])

    def need(*wanted):
        for n in wanted:
            loads.pop(n).wait()

    def row(n):
        return vm[n][...].reshape(1, -1)

    def send(stage, level, which, source, target, plan):
        devices = (takers if stage < 2 else owners)[level]
        copies = {}
        for i in which:
            start, place, rows, neighbour = plan[i]
            copies[i] = pltpu.make_async_remote_copy(
                src_ref=source.at[level, pl.ds(start, rows)],
                dst_ref=target.at[level, pl.ds(place, rows)],
                send_sem=send_sem.at[stage, level, i],
                recv_sem=recv_sem.at[stage, level, i],
                device_id=devices[neighbour],
                device_id_type=MESH,
            )
            copies[i].start()
        return copies

    need("send1")
    for level in range(2):
        need(("tokens", level))
        snd1[level] = dot(vm["send1"][level], buf1[level, 0:OWN]).astype(BF)
    pl.semaphore_wait(barrier, 8)
    one = [{}, {}]
    for i in range(3):
        for level in range(2):
            one[level].update(send(0, level, (i,), snd1, buf1, TOKENS))
    load(*order[len(EARLY):])

    need("qkv_weight", "far")
    zero = jnp.zeros((C, 64), BF)
    for part in range(3):
        qkv_pad[:, part * 256 : part * 256 + C] = vm["qkv_weight"][:, part * C : (part + 1) * C]
        qkv_pad[:, part * 256 + C : (part + 1) * 256] = zero
    edge = (lat_n - 1, 0)
    for level in range(2):
        far_v[level] = jnp.where(lat == edge[level], vm["far"][...].astype(F32), 0.0)
    need("norm_gain", "ones4", "ones2", "proj_weight", "gather1")
    lane = lax.broadcasted_iota(jnp.int32, (PAD, 128), 1)
    masks = [jnp.where(lane // HEAD == h, 1.0, 0.0).astype(BF) for h in range(4)]
    ones4, ones2 = vm["ones4"], vm["ones2"]

    def fine(tokens, items):
        normed, scale = centre(tokens, row("norm_gain"))
        packed = dot(normed, qkv_pad[...]) * scale
        q = (packed[:, 0:256] * Q_SCALE).astype(BF)
        k = packed[:, 256:512].astype(BF)
        v = packed[:, 512:768].astype(BF)
        heads = []
        for i, (level, w) in enumerate(items):
            at = slice(i * PAD, (i + 1) * PAD)
            far = far_v[level, 3 - w] if w >= 2 else None
            heads.append(attend6(q[at], k[at], v[at], ones4[...], ones2[...], masks, far))
        heads = jnp.concatenate(heads, axis=0)[:, 0:C]
        result = (tokens + dot(heads, vm["proj_weight"][...])).astype(BF)
        for i, (level, w) in enumerate(items):
            buf2[level, w * PAD : (w + 1) * PAD] = result[i * PAD : (i + 1) * PAD]

    first = [dot(vm["gather1"][level, 0:PAD, 0:OWN], buf1[level, 0:OWN]) for level in range(2)]
    fine(jnp.concatenate(first, axis=0), [(0, 0), (1, 0)])

    two = [send(1, level, (0, 1, 2), buf2, buf2, RESULTS) for level in range(2)]

    for level in range(2):
        one[level][0].wait_recv()
    rest = []
    for level in range(2):
        own = dot(vm["gather1"][level, PAD : 2 * PAD, 0:OWN], buf1[level, 0:OWN])
        table = vm["gather1"][level, PAD : 2 * PAD, OWN : OWN + DIAG_AT]
        rest.append(own + dot(table[:, LON_AT:DIAG_AT], buf1[level, OWN + LON_AT : OWN + DIAG_AT]))
    fine(jnp.concatenate(rest, axis=0), [(0, 1), (1, 1)])
    for level in range(2):
        two[level].update(send(1, level, (3,), buf2, buf2, RESULTS))
    near = OWN + LON_AT
    for level in range(2):
        one[level][1].wait_recv()
    rest = [dot(vm["gather1"][level, 2 * PAD : 3 * PAD, 0:near], buf1[level, 0:near]) for level in range(2)]
    fine(jnp.concatenate(rest, axis=0), [(0, 2), (1, 2)])
    for level in range(2):
        two[level].update(send(1, level, (4,), buf2, buf2, RESULTS))
    for level in range(2):
        one[level][2].wait_recv()
    last = [dot(vm["gather1"][level, 3 * PAD : 4 * PAD], buf1[level]) for level in range(2)]
    fine(jnp.concatenate(last, axis=0), [(0, 3), (1, 3)])

    need("up_weight")
    for k in range(4):
        up_pad[:, k * 256 : k * 256 + C] = vm["up_weight"][:, k * C : (k + 1) * C]
    need("gather2", "send3", "merge_gain", "merge_weight", "coarse_gain", "coarse_qkv", "coarse_proj")
    need("up_gain", "out_weight", "final")

    for level in range(2):
        for copy in two[level].values():
            copy.wait_recv()
    cells = [dot(vm["gather2"][...], buf2[level]) for level in range(2)]
    group = [
        jnp.concatenate([cells[level][(k ^ m) * PAD : ((k ^ m) + 1) * PAD] for level, m in enumerate(MIRROR)], axis=0)
        for k in range(4)
    ]
    average = jnp.sum(group[0] + group[1] + group[2] + group[3], axis=-1, keepdims=True) * (1.0 / (4 * C))
    centred = [g - average for g in group]
    squares = [c * c for c in centred]
    spread = jnp.sum(squares[0] + squares[1] + squares[2] + squares[3], axis=-1, keepdims=True) * (1.0 / (4 * C))
    scale = lax.rsqrt(spread + EPSILON)
    coarse = jnp.zeros((2 * PAD, CC), F32)
    for k in range(4):
        stacked = (centred[k] * row("merge_gain")[:, k * C : (k + 1) * C]).astype(BF)
        coarse = coarse + dot(stacked, vm["merge_weight"][k * C : (k + 1) * C])
    coarse = (coarse * scale).astype(BF).astype(F32)
    normed, scale = centre(coarse, row("coarse_gain"))
    packed = dot(normed, vm["coarse_qkv"][...]) * scale
    q = (packed[:, 0:CC] * Q_SCALE).astype(BF)
    k = packed[:, CC : 2 * CC].astype(BF)
    v = packed[:, 2 * CC : 3 * CC].astype(BF)
    heads = []
    for level in range(2):
        at = slice(level * PAD, (level + 1) * PAD)
        parts = []
        for j in range(3):
            cut = slice(j * 128, (j + 1) * 128)
            far = far_v[level, 0, :, 0 : 4 * PAD]
            parts.append(attend4(q[at, cut], k[at, cut], v[at, cut], ones4[...], masks, far).astype(BF))
        heads.append(jnp.concatenate(parts, axis=1))
    heads = jnp.concatenate(heads, axis=0)
    coarse_out = (coarse + dot(heads, vm["coarse_proj"][...])).astype(BF)
    lifted = [dot(coarse_out, up_pad[:, k * 256 : k * 256 + C]) for k in range(4)]
    normed = [centre(x, row("up_gain")) for x in lifted]
    branch = dot(jnp.concatenate([n for n, _ in normed], axis=0), vm["out_weight"][...])
    encoded = [(group[k] + branch[k * 2 * PAD : (k + 1) * 2 * PAD] * normed[k][1]).astype(BF) for k in range(4)]
    three, mines = [], []
    for level in range(2):
        mine = [encoded[k ^ MIRROR[level]][level * PAD : (level + 1) * PAD] for k in range(4)]
        mine = jnp.concatenate(mine, axis=0)
        snd3[level] = dot(vm["send3"][PAD : 4 * PAD], mine).astype(BF)
        three.append(send(2, level, (0, 1, 2), snd3, buf3, ENCODED))
        mines.append(mine)
    for level in range(2):
        buf3[level, 0:PAD] = dot(vm["send3"][0:PAD], mines[level]).astype(BF)

    for level in range(2):
        for copy in three[level].values():
            copy.wait_recv()
        out_ref[level] = dot(vm["final"][level], buf3[level]).astype(BF)
    for copies in one + two + three:
        for copy in copies.values():
            copy.wait_send()


def body(lat_n, lon_n, tokens, norm_gain, qkv_weight, proj_weight, merge_gain, merge_weight, coarse_gain, *rest):
    coarse_qkv, coarse_proj, up_weight, up_gain, out_weight = rest
    table = tables()
    args = [
        tokens.reshape(2, OWN, C),
        norm_gain,
        qkv_weight,
        proj_weight,
        merge_gain,
        merge_weight,
        coarse_gain,
        coarse_qkv,
        coarse_proj,
        up_weight,
        up_gain,
        out_weight,
    ] + [jnp.asarray(table[n]) for n in TABLES]
    scratch = [pltpu.VMEM(a.shape, a.dtype) for a in args[1:]]
    scratch += [
        pltpu.VMEM((C, 768), BF),
        pltpu.VMEM((CC, 1024), BF),
        pltpu.VMEM((2, 2, PAD, 6 * PAD), F32),
        pltpu.VMEM((2, OWN + HALO, C), BF),
        pltpu.VMEM((2, 4 * PAD + HALO2, C), BF),
        pltpu.VMEM((2, 4 * PAD, C), BF),
        pltpu.VMEM((2, HALO, C), BF),
        pltpu.VMEM((2, 3 * PAD, C), BF),
        pltpu.SemaphoreType.DMA((len(args) - 1,)),
        pltpu.SemaphoreType.DMA((2,)),
        pltpu.SemaphoreType.DMA((3, 2, 5)),
        pltpu.SemaphoreType.DMA((3, 2, 5)),
    ]
    out = pl.pallas_call(
        functools.partial(kernel, lat_n, lon_n),
        out_shape=jax.ShapeDtypeStruct((2, OWN, C), BF),
        in_specs=[pl.BlockSpec(memory_space=pltpu.HBM)] * len(args),
        out_specs=pl.BlockSpec(memory_space=pltpu.VMEM),
        scratch_shapes=scratch,
        compiler_params=pltpu.CompilerParams(
            collective_id=0, has_side_effects=True, vmem_limit_bytes=40 * 1024 * 1024
        ),
    )(*[pltpu.with_memory_space_constraint(a, pltpu.HBM) for a in args])
    return out.reshape(tokens.shape)


def solution(mesh):
    placed = (P(None, "lat", "lon", None),) + (P(),) * 11
    return jax.shard_map(
        functools.partial(body, mesh.shape["lat"], mesh.shape["lon"]),
        mesh=mesh,
        in_specs=placed,
        out_specs=P(None, "lat", "lon", None),
        check_vma=False,
    )
```

```python
import functools

import jax
import jax.numpy as jnp
import ml_dtypes
import numpy as np
from jax import lax
from jax.experimental import pallas as pl
from jax.experimental.pallas import tpu as pltpu
from jax.sharding import PartitionSpec as P

MESH = pl.DeviceIdType.MESH
BF = jnp.bfloat16
F32 = jnp.float32
EPSILON = 1e-05
C = 192
CC = 384
ROWS, COLS = 12, 24
OWN = ROWS * COLS
UNIT = 18
WIN = 72
PAD = 80
HEAD = 32
Q_SCALE = float(HEAD**-0.5 * np.log2(np.e))
V_SCALE = 2.0**-8
FAR = -1e30
HALO = 176
LAT_AT, LON_AT, LON_LAST, DIAG_AT = 0, 64, 112, 144
HALO2 = 192
MIRROR = (2, 3)
SOON = 4 * PAD + 144
RESULTS = (
    (0, 4 * PAD, 32, 2),
    (16, 4 * PAD + 32, 32, 0),
    (32, 4 * PAD + 64, 32, 1),
    (PAD, 4 * PAD + 144, 48, 0),
    (2 * PAD, 4 * PAD + 96, 48, 1),
)
TOKENS = (
    (LON_AT, OWN + LON_AT, 48, 1),
    (LAT_AT, OWN + LAT_AT, 64, 0),
    (DIAG_AT, OWN + DIAG_AT, 32, 2),
    (LON_LAST, OWN + LON_LAST, 32, 1),
)
ENCODED = ((2 * PAD, 2 * PAD, PAD, 2), (PAD, PAD, PAD, 0), (0, 0, PAD, 1))


def one_hot(rows, cols, pairs):
    out = np.zeros((rows, cols), np.float32)
    for r, c in pairs:
        out[r, c] = 1.0
    return out.astype(ml_dtypes.bfloat16)


def halo_slot():
    for j in range(3):
        yield LAT_AT + j * UNIT, (0, j + 1)
        yield (LON_LAST if j == 2 else LON_AT + j * UNIT), (j + 1, 0)
    yield DIAG_AT, (0, 0)


def received(a, b):
    if a == 3 and b == 3:
        return DIAG_AT
    if a == 3:
        return LAT_AT + b * UNIT
    if b == 3:
        return LON_LAST if a == 2 else LON_AT + a * UNIT
    return None


def window_row(a, b):
    window, inner = (a // 2) * 2 + b // 2, (a % 2) * 2 + b % 2
    if window == 2:
        inner = (b % 2) * 2 + a % 2
    return window * PAD + inner * UNIT


def arrival(a, b):
    if a < 3 and b < 3:
        return window_row(a + 1, b + 1)
    which = {(3, 0): 1, (3, 1): 3, (3, 2): 3, (0, 3): 2, (1, 3): 4, (2, 3): 4, (3, 3): 0}[a, b]
    theirs = window_row(0 if a == 3 else a + 1, 0 if b == 3 else b + 1)
    return RESULTS[which][1] + theirs - RESULTS[which][0]


def natural(level, r, c):
    return (r if level == 0 else ROWS - 1 - r) * COLS + COLS - 1 - c


@functools.cache
def tables():
    units = [(a, b) for a in range(4) for b in range(4)]
    send1, gather1, final = [], [], []
    for level in range(2):

        def own(a, b, t, level=level):
            return natural(level, a * 3 + t // 6, b * 6 + t % 6)

        send1.append(
            one_hot(HALO, OWN, [(s + t, own(a, b, t)) for s, (a, b) in halo_slot() for t in range(UNIT)])
        )
        pairs = []
        for a, b in units:
            slot = received(a, b)
            for t in range(UNIT):
                source = own(a + 1, b + 1, t) if slot is None else OWN + slot + t
                pairs.append((window_row(a, b) + t, source))
        gather1.append(one_hot(4 * PAD, OWN + HALO, pairs))
        pairs = []
        for r in range(ROWS):
            for c in range(COLS):
                qr, qc = int(r < 6), int(c < 12)
                y, x = r % 6, c % 12
                k = y % 2 + 2 * (x % 2)
                t = (y // 2) * 6 + x // 2
                pairs.append((natural(level, r, c), (qr * 2 + qc) * PAD + k * UNIT + t))
        final.append(one_hot(OWN, 4 * PAD, pairs))
    pairs = []
    for y in range(ROWS):
        for x in range(COLS):
            a, b, t = y // 3, x // 6, (y % 3) * 6 + x % 6
            source = arrival(a, b) + t
            k = y % 2 + 2 * (x % 2)
            i, j = y // 2, x // 2
            cell = ((i // 3) * 2 + j // 6) * UNIT + (i % 3) * 6 + j % 6
            pairs.append((k * PAD + cell, source))
    gather2 = one_hot(4 * PAD, 4 * PAD + HALO2, pairs)
    pairs = []
    for quarter in range(4):
        for k in range(4):
            for t in range(UNIT):
                pairs.append((quarter * PAD + k * UNIT + t, k * PAD + quarter * UNIT + t))
    send3 = one_hot(4 * PAD, 4 * PAD, pairs)
    ones4 = np.zeros((4 * PAD, 128), np.float32)
    ones2 = np.zeros((224, 128), np.float32)
    for h in range(4):
        ones4[h * PAD : h * PAD + WIN, h * HEAD : (h + 1) * HEAD] = 1.0
    for h in range(2):
        ones2[64 + h * PAD : 64 + h * PAD + WIN, h * HEAD : (h + 1) * HEAD] = 1.0
    ones2[64 : 64 + WIN, 2 * HEAD :] = 1.0
    far = []
    for by_column in (False, True):
        units_of = np.arange(PAD) // UNIT
        side = (units_of % 2 if by_column else units_of // 2) == 1
        far.append(np.where(side[:, None] != np.tile(side, 6)[None, :], np.float32(FAR), np.float32(0.0)))
    far = np.stack(far)
    return dict(
        send1=np.stack(send1),
        gather1=np.stack(gather1),
        gather2=gather2[:, 0:SOON],
        gather2b=gather2[:, SOON:],
        lon1=np.stack(gather1)[:, PAD : 2 * PAD, OWN + LON_AT : OWN + LON_LAST],
        send3=send3,
        final=np.stack(final)[:, :, 0:PAD],
        final_b=np.stack(final)[:, :, PAD:],
        ones4=ones4.astype(ml_dtypes.bfloat16),
        ones2=ones2.astype(ml_dtypes.bfloat16),
        far=far.astype(ml_dtypes.bfloat16),
    )


ARGUMENTS = ("tokens", "norm_gain", "qkv_weight", "proj_weight", "merge_gain", "merge_weight", "coarse_gain", "coarse_qkv")
ARGUMENTS += ("coarse_proj", "up_weight", "up_gain", "out_weight")
EARLY = ("send1", "norm_gain", "qkv_weight", "far", "ones4", "ones2", "proj_weight", "gather1", "lon1")
TABLES = ("send1", "gather1", "gather2", "gather2b", "lon1", "send3", "final", "final_b", "ones4", "ones2", "far")


def dot(a, b):
    return jnp.dot(a, b, preferred_element_type=F32)


def centre(values, gain):
    centred = values - jnp.mean(values, axis=-1, keepdims=True)
    spread = jnp.mean(centred * centred, axis=-1, keepdims=True)
    return (centred * gain).astype(BF), lax.rsqrt(spread + EPSILON)


def dot_t(a, b):
    return lax.dot_general(a, b, (((1,), (1,)), ((), ())), preferred_element_type=F32)


def shared(raised, values, ones):
    both = dot(raised, jnp.concatenate([values, ones], axis=1))
    return both[:, 0:128] / (both[:, 128:256] * V_SCALE)


def attend4(q, k, v, ones4, masks, far):
    keys = jnp.concatenate([k * m for m in masks], axis=0)
    raised = jnp.exp2(dot_t(q, keys) + far).astype(BF)
    small = v * jnp.bfloat16(V_SCALE)
    return shared(raised, jnp.concatenate([small * m for m in masks], axis=0), ones4)


def attend6(q, k, v, ones4, ones2, masks, far):
    zero = jnp.zeros((PAD, 128), BF)
    k0, k1 = k[:, 0:128], k[:, 128:256]
    keys = [jnp.concatenate([k0 * m, zero], axis=1) for m in masks]
    keys += [jnp.concatenate([zero, k1 * m], axis=1) for m in masks[0:2]]
    scores = dot_t(q, jnp.concatenate(keys, axis=0))
    if far is not None:
        scores = scores + far
    raised = jnp.exp2(scores).astype(BF)
    small = v * jnp.bfloat16(V_SCALE)
    v0, v1 = small[:, 0:128], small[:, 128:256]
    first = shared(raised[:, 0 : 4 * PAD], jnp.concatenate([v0 * m for m in masks], axis=0), ones4)
    last = [zero[0:64]] + [v1 * m for m in masks[0:2]]
    last = shared(raised[:, 256 : 6 * PAD], jnp.concatenate(last, axis=0), ones2)
    return jnp.concatenate([first, last], axis=1).astype(BF)


def kernel(lat_n, lon_n, *refs):
    names = list(ARGUMENTS)
    names += list(TABLES)
    hbm = dict(zip(names, refs))
    out_ref = refs[len(names)]
    scratch = refs[len(names) + 1 :]
    vm = dict(zip(names[1:], scratch))
    (qkv_pad, up_pad, far_v, buf1, buf2, buf3, snd1, snd3, load_sem, tok_sem, send_sem, recv_sem) = scratch[
        len(names) - 1 :
    ]

    lat, lon = lax.axis_index("lat"), lax.axis_index("lon")
    up, down = lax.rem(lat + 1, lat_n), lax.rem(lat + lat_n - 1, lat_n)
    east, west = lax.rem(lon + 1, lon_n), lax.rem(lon + lon_n - 1, lon_n)
    takers = (((down, lon), (lat, east), (down, east)), ((up, lon), (lat, east), (up, east)))
    owners = (((up, lon), (lat, west), (up, west)), ((down, lon), (lat, west), (down, west)))

    barrier = pltpu.get_barrier_semaphore()
    for device in ((up, lon), (down, lon), (lat, east), (lat, west)) + tuple((a, b) for a in (up, down) for b in (east, west)):
        pl.semaphore_signal(barrier, inc=1, device_id=device, device_id_type=MESH)

    loads = {}
    for level in range(2):
        loads["tokens", level] = pltpu.make_async_copy(
            hbm["tokens"].at[level], buf1.at[level, pl.ds(0, OWN)], tok_sem.at[level]
        )
        loads["tokens", level].start()
    order = ["send1"] + [n for n in EARLY if n != "send1"]
    order += [n for n in names[1:] if n not in order]

    def load(*wanted):
        for n in wanted:
            loads[n] = pltpu.make_async_copy(hbm[n], vm[n], load_sem.at[order.index(n)])
            loads[n].start()

    load(*order[:len(EARLY)])

    def need(*wanted):
        for n in wanted:
            loads.pop(n).wait()

    def row(n):
        return vm[n][...].reshape(1, -1)

    def send(stage, level, which, source, target, plan):
        devices = (takers if stage < 2 else owners)[level]
        copies = {}
        for i in which:
            start, place, rows, neighbour = plan[i]
            copies[i] = pltpu.make_async_remote_copy(
                src_ref=source.at[level, pl.ds(start, rows)],
                dst_ref=target.at[level, pl.ds(place, rows)],
                send_sem=send_sem.at[stage, level, i],
                recv_sem=recv_sem.at[stage, level, i],
                device_id=devices[neighbour],
                device_id_type=MESH,
            )
            copies[i].start()
        return copies

    need("send1")
    for level in range(2):
        need(("tokens", level))
        snd1[level] = dot(vm["send1"][level], buf1[level, 0:OWN]).astype(BF)
    pl.semaphore_wait(barrier, 8)
    one = [{}, {}]
    for i in (0, 1, 3, 2):
        for level in range(2):
            one[level].update(send(0, level, (i,), snd1, buf1, TOKENS))
    load(*order[len(EARLY):])

    need("qkv_weight", "far")
    zero = jnp.zeros((C, 64), BF)
    for part in range(3):
        qkv_pad[:, part * 256 : part * 256 + C] = vm["qkv_weight"][:, part * C : (part + 1) * C]
        qkv_pad[:, part * 256 + C : (part + 1) * 256] = zero
    edge = (lat_n - 1, 0)
    for level in range(2):
        far_v[level] = jnp.where(lat == edge[level], vm["far"][...].astype(F32), 0.0)
    need("norm_gain", "ones4", "ones2", "proj_weight", "gather1", "lon1")
    lane = lax.broadcasted_iota(jnp.int32, (PAD, 128), 1)
    masks = [jnp.where(lane // HEAD == h, 1.0, 0.0).astype(BF) for h in range(4)]
    ones4, ones2 = vm["ones4"], vm["ones2"]

    def fine(tokens, items):
        normed, scale = centre(tokens, row("norm_gain"))
        packed = dot(normed, qkv_pad[...]) * scale
        q = (packed[:, 0:256] * Q_SCALE).astype(BF)
        k = packed[:, 256:512].astype(BF)
        v = packed[:, 512:768].astype(BF)
        heads = []
        for i, (level, w) in enumerate(items):
            at = slice(i * PAD, (i + 1) * PAD)
            far = far_v[level, 3 - w] if w >= 2 else None
            heads.append(attend6(q[at], k[at], v[at], ones4[...], ones2[...], masks, far))
        heads = jnp.concatenate(heads, axis=0)[:, 0:C]
        result = (tokens + dot(heads, vm["proj_weight"][...])).astype(BF)
        for i, (level, w) in enumerate(items):
            buf2[level, w * PAD : (w + 1) * PAD] = result[i * PAD : (i + 1) * PAD]

    first = [dot(vm["gather1"][level, 0:PAD, 0:OWN], buf1[level, 0:OWN]) for level in range(2)]
    fine(jnp.concatenate(first, axis=0), [(0, 0), (1, 0)])

    two = [send(1, level, (0, 1, 2), buf2, buf2, RESULTS) for level in range(2)]

    own = [dot(vm["gather1"][level, PAD : 2 * PAD, 0:OWN], buf1[level, 0:OWN]) for level in range(2)]
    for level in range(2):
        one[level][0].wait_recv()
    near, nearer = OWN + LON_AT, OWN + LON_LAST
    rest = [own[level] + dot(vm["lon1"][level], buf1[level, near:nearer]) for level in range(2)]
    fine(jnp.concatenate(rest, axis=0), [(0, 1), (1, 1)])
    for level in range(2):
        two[level].update(send(1, level, (3,), buf2, buf2, RESULTS))
    near = OWN + LON_AT
    for level in range(2):
        one[level][1].wait_recv()
    rest = [dot(vm["gather1"][level, 2 * PAD : 3 * PAD, 0:near], buf1[level, 0:near]) for level in range(2)]
    fine(jnp.concatenate(rest, axis=0), [(0, 2), (1, 2)])
    for level in range(2):
        two[level].update(send(1, level, (4,), buf2, buf2, RESULTS))
    for level in range(2):
        one[level][3].wait_recv()
        one[level][2].wait_recv()
    last = [dot(vm["gather1"][level, 3 * PAD : 4 * PAD], buf1[level]) for level in range(2)]
    fine(jnp.concatenate(last, axis=0), [(0, 3), (1, 3)])

    need("up_weight")
    for k in range(4):
        up_pad[:, k * 256 : k * 256 + C] = vm["up_weight"][:, k * C : (k + 1) * C]
    need("gather2", "send3", "merge_gain", "merge_weight", "coarse_gain", "coarse_qkv", "coarse_proj")
    need("up_gain", "out_weight", "final", "final_b", "gather2b")

    for level in range(2):
        for i in (0, 1, 2, 4):
            two[level][i].wait_recv()
    soon = [dot(vm["gather2"][...], buf2[level, 0:SOON]) for level in range(2)]
    for level in range(2):
        two[level][3].wait_recv()
    cells = [soon[level] + dot(vm["gather2b"][...], buf2[level, SOON:]) for level in range(2)]
    group = [
        jnp.concatenate([cells[level][(k ^ m) * PAD : ((k ^ m) + 1) * PAD] for level, m in enumerate(MIRROR)], axis=0)
        for k in range(4)
    ]
    average = jnp.sum(group[0] + group[1] + group[2] + group[3], axis=-1, keepdims=True) * (1.0 / (4 * C))
    centred = [g - average for g in group]
    squares = [c * c for c in centred]
    spread = jnp.sum(squares[0] + squares[1] + squares[2] + squares[3], axis=-1, keepdims=True) * (1.0 / (4 * C))
    scale = lax.rsqrt(spread + EPSILON)
    coarse = jnp.zeros((2 * PAD, CC), F32)
    for k in range(4):
        stacked = (centred[k] * row("merge_gain")[:, k * C : (k + 1) * C]).astype(BF)
        coarse = coarse + dot(stacked, vm["merge_weight"][k * C : (k + 1) * C])
    coarse = (coarse * scale).astype(BF).astype(F32)
    normed, scale = centre(coarse, row("coarse_gain"))
    packed = dot(normed, vm["coarse_qkv"][...]) * scale
    q = (packed[:, 0:CC] * Q_SCALE).astype(BF)
    k = packed[:, CC : 2 * CC].astype(BF)
    v = packed[:, 2 * CC : 3 * CC].astype(BF)
    heads = []
    for level in range(2):
        at = slice(level * PAD, (level + 1) * PAD)
        parts = []
        for j in range(3):
            cut = slice(j * 128, (j + 1) * 128)
            far = far_v[level, 0, :, 0 : 4 * PAD]
            parts.append(attend4(q[at, cut], k[at, cut], v[at, cut], ones4[...], masks, far).astype(BF))
        heads.append(jnp.concatenate(parts, axis=1))
    heads = jnp.concatenate(heads, axis=0)
    coarse_out = (coarse + dot(heads, vm["coarse_proj"][...])).astype(BF)
    lifted = [dot(coarse_out, up_pad[:, k * 256 : k * 256 + C]) for k in range(4)]
    normed = [centre(x, row("up_gain")) for x in lifted]
    branch = dot(jnp.concatenate([n for n, _ in normed], axis=0), vm["out_weight"][...])
    encoded = [(group[k] + branch[k * 2 * PAD : (k + 1) * 2 * PAD] * normed[k][1]).astype(BF) for k in range(4)]
    three, mines = [], []
    for level in range(2):
        mine = [encoded[k ^ MIRROR[level]][level * PAD : (level + 1) * PAD] for k in range(4)]
        mine = jnp.concatenate(mine, axis=0)
        snd3[level] = dot(vm["send3"][PAD : 4 * PAD], mine).astype(BF)
        three.append(send(2, level, (0, 1, 2), snd3, buf3, ENCODED))
        mines.append(mine)
    mines = [dot(vm["send3"][0:PAD], mine).astype(BF) for mine in mines]
    mines = [dot(vm["final"][level], mines[level]) for level in range(2)]
    for level in range(2):
        for copy in three[level].values():
            copy.wait_recv()
        out_ref[level] = (mines[level] + dot(vm["final_b"][level], buf3[level])).astype(BF)
    for copies in one + two + three:
        for copy in copies.values():
            copy.wait_send()


def body(lat_n, lon_n, tokens, norm_gain, qkv_weight, proj_weight, merge_gain, merge_weight, coarse_gain, *rest):
    coarse_qkv, coarse_proj, up_weight, up_gain, out_weight = rest
    table = tables()
    args = [
        tokens.reshape(2, OWN, C),
        norm_gain,
        qkv_weight,
        proj_weight,
        merge_gain,
        merge_weight,
        coarse_gain,
        coarse_qkv,
        coarse_proj,
        up_weight,
        up_gain,
        out_weight,
    ] + [jnp.asarray(table[n]) for n in TABLES]
    scratch = [pltpu.VMEM(a.shape, a.dtype) for a in args[1:]]
    scratch += [
        pltpu.VMEM((C, 768), BF),
        pltpu.VMEM((CC, 1024), BF),
        pltpu.VMEM((2, 2, PAD, 6 * PAD), F32),
        pltpu.VMEM((2, OWN + HALO, C), BF),
        pltpu.VMEM((2, 4 * PAD + HALO2, C), BF),
        pltpu.VMEM((2, 3 * PAD, C), BF),
        pltpu.VMEM((2, HALO, C), BF),
        pltpu.VMEM((2, 3 * PAD, C), BF),
        pltpu.SemaphoreType.DMA((len(args) - 1,)),
        pltpu.SemaphoreType.DMA((2,)),
        pltpu.SemaphoreType.DMA((3, 2, 5)),
        pltpu.SemaphoreType.DMA((3, 2, 5)),
    ]
    out = pl.pallas_call(
        functools.partial(kernel, lat_n, lon_n),
        out_shape=jax.ShapeDtypeStruct((2, OWN, C), BF),
        in_specs=[pl.BlockSpec(memory_space=pltpu.HBM)] * len(args),
        out_specs=pl.BlockSpec(memory_space=pltpu.VMEM),
        scratch_shapes=scratch,
        compiler_params=pltpu.CompilerParams(
            collective_id=0, has_side_effects=True, vmem_limit_bytes=40 * 1024 * 1024
        ),
    )(*[pltpu.with_memory_space_constraint(a, pltpu.HBM) for a in args])
    return out.reshape(tokens.shape)


def solution(mesh):
    placed = (P(None, "lat", "lon", None),) + (P(),) * 11
    return jax.shard_map(
        functools.partial(body, mesh.shape["lat"], mesh.shape["lon"]),
        mesh=mesh,
        in_specs=placed,
        out_specs=P(None, "lat", "lon", None),
        check_vma=False,
    )
```

```python
import functools

import jax
import jax.numpy as jnp
import ml_dtypes
import numpy as np
from jax import lax
from jax.experimental import pallas as pl
from jax.experimental.pallas import tpu as pltpu
from jax.sharding import PartitionSpec as P

MESH = pl.DeviceIdType.MESH
BF = jnp.bfloat16
F32 = jnp.float32
EPSILON = 1e-05
C = 192
CC = 384
ROWS, COLS = 12, 24
OWN = ROWS * COLS
UNIT = 18
WIN = 72
PAD = 80
HEAD = 32
Q_SCALE = float(HEAD**-0.5 * np.log2(np.e))
V_SCALE = 2.0**-8
FAR = -1e30
HALO = 176
LAT_AT, LON_AT, LON_LAST, DIAG_AT = 0, 64, 112, 144
HALO2 = 192
MIRROR = (2, 3)
SOON = 4 * PAD + 144
RESULTS = (
    (0, 4 * PAD, 32, 2),
    (16, 4 * PAD + 32, 32, 0),
    (32, 4 * PAD + 64, 32, 1),
    (PAD, 4 * PAD + 144, 48, 0),
    (2 * PAD, 4 * PAD + 96, 48, 1),
)
TOKENS = (
    (LON_AT, OWN + LON_AT, 48, 1),
    (LAT_AT, OWN + LAT_AT, 64, 0),
    (DIAG_AT, OWN + DIAG_AT, 32, 2),
    (LON_LAST, OWN + LON_LAST, 32, 1),
)
ENCODED = ((PAD, PAD, PAD, 0), (2 * PAD, 2 * PAD, PAD, 2), (0, 0, PAD, 1))


def one_hot(rows, cols, pairs):
    out = np.zeros((rows, cols), np.float32)
    for r, c in pairs:
        out[r, c] = 1.0
    return out.astype(ml_dtypes.bfloat16)


def halo_slot():
    for j in range(3):
        yield LAT_AT + j * UNIT, (0, j + 1)
        yield (LON_LAST if j == 2 else LON_AT + j * UNIT), (j + 1, 0)
    yield DIAG_AT, (0, 0)


def received(a, b):
    if a == 3 and b == 3:
        return DIAG_AT
    if a == 3:
        return LAT_AT + b * UNIT
    if b == 3:
        return LON_LAST if a == 2 else LON_AT + a * UNIT
    return None


def window_row(a, b):
    window, inner = (a // 2) * 2 + b // 2, (a % 2) * 2 + b % 2
    if window == 2:
        inner = (b % 2) * 2 + a % 2
    return window * PAD + inner * UNIT


def arrival(a, b):
    if a < 3 and b < 3:
        return window_row(a + 1, b + 1)
    which = {(3, 0): 1, (3, 1): 3, (3, 2): 3, (0, 3): 2, (1, 3): 4, (2, 3): 4, (3, 3): 0}[a, b]
    theirs = window_row(0 if a == 3 else a + 1, 0 if b == 3 else b + 1)
    return RESULTS[which][1] + theirs - RESULTS[which][0]


def natural(level, r, c):
    return (r if level == 0 else ROWS - 1 - r) * COLS + COLS - 1 - c


@functools.cache
def tables():
    units = [(a, b) for a in range(4) for b in range(4)]
    send1, gather1, final = [], [], []
    for level in range(2):

        def own(a, b, t, level=level):
            return natural(level, a * 3 + t // 6, b * 6 + t % 6)

        send1.append(
            one_hot(HALO, OWN, [(s + t, own(a, b, t)) for s, (a, b) in halo_slot() for t in range(UNIT)])
        )
        pairs = []
        for a, b in units:
            slot = received(a, b)
            for t in range(UNIT):
                source = own(a + 1, b + 1, t) if slot is None else OWN + slot + t
                pairs.append((window_row(a, b) + t, source))
        gather1.append(one_hot(4 * PAD, OWN + HALO, pairs))
        pairs = []
        for r in range(ROWS):
            for c in range(COLS):
                qr, qc = int(r < 6), int(c < 12)
                y, x = r % 6, c % 12
                k = y % 2 + 2 * (x % 2)
                t = (y // 2) * 6 + x // 2
                pairs.append((natural(level, r, c), (qr * 2 + qc) * PAD + k * UNIT + t))
        final.append(one_hot(OWN, 4 * PAD, pairs))
    pairs = []
    for y in range(ROWS):
        for x in range(COLS):
            a, b, t = y // 3, x // 6, (y % 3) * 6 + x % 6
            source = arrival(a, b) + t
            k = y % 2 + 2 * (x % 2)
            i, j = y // 2, x // 2
            cell = ((i // 3) * 2 + j // 6) * UNIT + (i % 3) * 6 + j % 6
            pairs.append((k * PAD + cell, source))
    gather2 = one_hot(4 * PAD, 4 * PAD + HALO2, pairs)
    pairs = []
    for quarter in range(4):
        for k in range(4):
            for t in range(UNIT):
                pairs.append((quarter * PAD + k * UNIT + t, k * PAD + quarter * UNIT + t))
    send3 = one_hot(4 * PAD, 4 * PAD, pairs)
    ones4 = np.zeros((4 * PAD, 128), np.float32)
    ones2 = np.zeros((224, 128), np.float32)
    for h in range(4):
        ones4[h * PAD : h * PAD + WIN, h * HEAD : (h + 1) * HEAD] = 1.0
    for h in range(2):
        ones2[64 + h * PAD : 64 + h * PAD + WIN, h * HEAD : (h + 1) * HEAD] = 1.0
    ones2[64 : 64 + WIN, 2 * HEAD :] = 1.0
    far = []
    for by_column in (False, True):
        units_of = np.arange(PAD) // UNIT
        side = (units_of % 2 if by_column else units_of // 2) == 1
        far.append(np.where(side[:, None] != np.tile(side, 6)[None, :], np.float32(FAR), np.float32(0.0)))
    far = np.stack(far)
    return dict(
        send1=np.stack(send1),
        gather1=np.stack(gather1),
        gather2=gather2[:, 0:SOON],
        gather2b=gather2[:, SOON:],
        lon1=np.stack(gather1)[:, PAD : 2 * PAD, OWN + LON_AT : OWN + LON_LAST],
        send3=send3,
        final=np.stack(final)[:, :, 0:PAD],
        final_b=np.stack(final)[:, :, PAD:],
        ones4=ones4.astype(ml_dtypes.bfloat16),
        ones2=ones2.astype(ml_dtypes.bfloat16),
        far=far.astype(ml_dtypes.bfloat16),
    )


ARGUMENTS = ("tokens", "norm_gain", "qkv_weight", "proj_weight", "merge_gain", "merge_weight", "coarse_gain", "coarse_qkv")
ARGUMENTS += ("coarse_proj", "up_weight", "up_gain", "out_weight")
EARLY = ("send1", "norm_gain", "qkv_weight", "far", "ones4", "ones2", "proj_weight", "gather1", "lon1")
TABLES = ("send1", "gather1", "gather2", "gather2b", "lon1", "send3", "final", "final_b", "ones4", "ones2", "far")


def dot(a, b):
    return jnp.dot(a, b, preferred_element_type=F32)


def centre(values, gain):
    centred = values - jnp.mean(values, axis=-1, keepdims=True)
    spread = jnp.mean(centred * centred, axis=-1, keepdims=True)
    return (centred * gain).astype(BF), lax.rsqrt(spread + EPSILON)


def dot_t(a, b):
    return lax.dot_general(a, b, (((1,), (1,)), ((), ())), preferred_element_type=F32)


def shared(raised, values, ones):
    both = dot(raised, jnp.concatenate([values, ones], axis=1))
    return both[:, 0:128] / (both[:, 128:256] * V_SCALE)


def attend4(q, k, v, ones4, masks, far):
    keys = jnp.concatenate([k * m for m in masks], axis=0)
    raised = jnp.exp2(dot_t(q, keys) + far).astype(BF)
    small = v * jnp.bfloat16(V_SCALE)
    return shared(raised, jnp.concatenate([small * m for m in masks], axis=0), ones4)


def attend6(q, k, v, ones4, ones2, masks, far):
    zero = jnp.zeros((PAD, 128), BF)
    k0, k1 = k[:, 0:128], k[:, 128:256]
    keys = [jnp.concatenate([k0 * m, zero], axis=1) for m in masks]
    keys += [jnp.concatenate([zero, k1 * m], axis=1) for m in masks[0:2]]
    scores = dot_t(q, jnp.concatenate(keys, axis=0))
    if far is not None:
        scores = scores + far
    raised = jnp.exp2(scores).astype(BF)
    small = v * jnp.bfloat16(V_SCALE)
    v0, v1 = small[:, 0:128], small[:, 128:256]
    first = shared(raised[:, 0 : 4 * PAD], jnp.concatenate([v0 * m for m in masks], axis=0), ones4)
    last = [zero[0:64]] + [v1 * m for m in masks[0:2]]
    last = shared(raised[:, 256 : 6 * PAD], jnp.concatenate(last, axis=0), ones2)
    return jnp.concatenate([first, last], axis=1).astype(BF)


def kernel(lat_n, lon_n, *refs):
    names = list(ARGUMENTS)
    names += list(TABLES)
    hbm = dict(zip(names, refs))
    out_ref = refs[len(names)]
    scratch = refs[len(names) + 1 :]
    vm = dict(zip(names[1:], scratch))
    (qkv_pad, up_pad, far_v, buf1, buf2, buf3, snd1, snd3, load_sem, tok_sem, send_sem, recv_sem) = scratch[
        len(names) - 1 :
    ]

    lat, lon = lax.axis_index("lat"), lax.axis_index("lon")
    up, down = lax.rem(lat + 1, lat_n), lax.rem(lat + lat_n - 1, lat_n)
    east, west = lax.rem(lon + 1, lon_n), lax.rem(lon + lon_n - 1, lon_n)
    takers = (((down, lon), (lat, east), (down, east)), ((up, lon), (lat, east), (up, east)))
    owners = (((up, lon), (lat, west), (up, west)), ((down, lon), (lat, west), (down, west)))

    barrier = pltpu.get_barrier_semaphore()
    for device in ((up, lon), (down, lon), (lat, east), (lat, west)) + tuple((a, b) for a in (up, down) for b in (east, west)):
        pl.semaphore_signal(barrier, inc=1, device_id=device, device_id_type=MESH)

    loads = {}
    for level in range(2):
        loads["tokens", level] = pltpu.make_async_copy(
            hbm["tokens"].at[level], buf1.at[level, pl.ds(0, OWN)], tok_sem.at[level]
        )
        loads["tokens", level].start()
    order = ["send1"] + [n for n in EARLY if n != "send1"]
    order += [n for n in names[1:] if n not in order]

    def load(*wanted):
        for n in wanted:
            loads[n] = pltpu.make_async_copy(hbm[n], vm[n], load_sem.at[order.index(n)])
            loads[n].start()

    load(*order)

    def need(*wanted):
        for n in wanted:
            loads.pop(n).wait()

    def row(n):
        return vm[n][...].reshape(1, -1)

    def send(stage, level, which, source, target, plan):
        devices = (takers if stage < 2 else owners)[level]
        copies = {}
        for i in which:
            start, place, rows, neighbour = plan[i]
            copies[i] = pltpu.make_async_remote_copy(
                src_ref=source.at[level, pl.ds(start, rows)],
                dst_ref=target.at[level, pl.ds(place, rows)],
                send_sem=send_sem.at[stage, level, i],
                recv_sem=recv_sem.at[stage, level, i],
                device_id=devices[neighbour],
                device_id_type=MESH,
            )
            copies[i].start()
        return copies

    need("send1")
    for level in range(2):
        need(("tokens", level))
        snd1[level] = dot(vm["send1"][level], buf1[level, 0:OWN]).astype(BF)
    pl.semaphore_wait(barrier, 8)
    one = [{}, {}]
    for i in (0, 1, 3, 2):
        for level in range(2):
            one[level].update(send(0, level, (i,), snd1, buf1, TOKENS))

    need("qkv_weight", "far")
    zero = jnp.zeros((C, 64), BF)
    for part in range(3):
        qkv_pad[:, part * 256 : part * 256 + C] = vm["qkv_weight"][:, part * C : (part + 1) * C]
        qkv_pad[:, part * 256 + C : (part + 1) * 256] = zero
    edge = (lat_n - 1, 0)
    for level in range(2):
        far_v[level] = jnp.where(lat == edge[level], vm["far"][...].astype(F32), 0.0)
    need("norm_gain", "ones4", "ones2", "proj_weight", "gather1", "lon1")
    lane = lax.broadcasted_iota(jnp.int32, (PAD, 128), 1)
    masks = [jnp.where(lane // HEAD == h, 1.0, 0.0).astype(BF) for h in range(4)]
    ones4, ones2 = vm["ones4"], vm["ones2"]

    def fine(tokens, items):
        normed, scale = centre(tokens, row("norm_gain"))
        packed = dot(normed, qkv_pad[...]) * scale
        q = (packed[:, 0:256] * Q_SCALE).astype(BF)
        k = packed[:, 256:512].astype(BF)
        v = packed[:, 512:768].astype(BF)
        heads = []
        for i, (level, w) in enumerate(items):
            at = slice(i * PAD, (i + 1) * PAD)
            far = far_v[level, 3 - w] if w >= 2 else None
            heads.append(attend6(q[at], k[at], v[at], ones4[...], ones2[...], masks, far))
        heads = jnp.concatenate(heads, axis=0)[:, 0:C]
        result = (tokens + dot(heads, vm["proj_weight"][...])).astype(BF)
        for i, (level, w) in enumerate(items):
            buf2[level, w * PAD : (w + 1) * PAD] = result[i * PAD : (i + 1) * PAD]

    first = [dot(vm["gather1"][level, 0:PAD, 0:OWN], buf1[level, 0:OWN]) for level in range(2)]
    fine(jnp.concatenate(first, axis=0), [(0, 0), (1, 0)])

    two = [send(1, level, (0, 1, 2), buf2, buf2, RESULTS) for level in range(2)]

    own = [dot(vm["gather1"][level, PAD : 2 * PAD, 0:OWN], buf1[level, 0:OWN]) for level in range(2)]
    for level in range(2):
        one[level][0].wait_recv()
    near, nearer = OWN + LON_AT, OWN + LON_LAST
    rest = [own[level] + dot(vm["lon1"][level], buf1[level, near:nearer]) for level in range(2)]
    fine(jnp.concatenate(rest, axis=0), [(0, 1), (1, 1)])
    for level in range(2):
        two[level].update(send(1, level, (3,), buf2, buf2, RESULTS))
    near = OWN + LON_AT
    for level in range(2):
        one[level][1].wait_recv()
    rest = [dot(vm["gather1"][level, 2 * PAD : 3 * PAD, 0:near], buf1[level, 0:near]) for level in range(2)]
    fine(jnp.concatenate(rest, axis=0), [(0, 2), (1, 2)])
    for level in range(2):
        two[level].update(send(1, level, (4,), buf2, buf2, RESULTS))
    for level in range(2):
        one[level][3].wait_recv()
        one[level][2].wait_recv()
    last = [dot(vm["gather1"][level, 3 * PAD : 4 * PAD], buf1[level]) for level in range(2)]
    fine(jnp.concatenate(last, axis=0), [(0, 3), (1, 3)])

    need("up_weight")
    for k in range(4):
        up_pad[:, k * 256 : k * 256 + C] = vm["up_weight"][:, k * C : (k + 1) * C]
    need("gather2", "send3", "merge_gain", "merge_weight", "coarse_gain", "coarse_qkv", "coarse_proj")
    need("up_gain", "out_weight", "final", "final_b", "gather2b")

    for level in range(2):
        for i in (0, 1, 2, 4):
            two[level][i].wait_recv()
    soon = [dot(vm["gather2"][...], buf2[level, 0:SOON]) for level in range(2)]
    for level in range(2):
        two[level][3].wait_recv()
    cells = [soon[level] + dot(vm["gather2b"][...], buf2[level, SOON:]) for level in range(2)]
    group = [
        jnp.concatenate([cells[level][(k ^ m) * PAD : ((k ^ m) + 1) * PAD] for level, m in enumerate(MIRROR)], axis=0)
        for k in range(4)
    ]
    average = jnp.sum(group[0] + group[1] + group[2] + group[3], axis=-1, keepdims=True) * (1.0 / (4 * C))
    centred = [g - average for g in group]
    squares = [c * c for c in centred]
    spread = jnp.sum(squares[0] + squares[1] + squares[2] + squares[3], axis=-1, keepdims=True) * (1.0 / (4 * C))
    scale = lax.rsqrt(spread + EPSILON)
    coarse = jnp.zeros((2 * PAD, CC), F32)
    for k in range(4):
        stacked = (centred[k] * row("merge_gain")[:, k * C : (k + 1) * C]).astype(BF)
        coarse = coarse + dot(stacked, vm["merge_weight"][k * C : (k + 1) * C])
    coarse = (coarse * scale).astype(BF).astype(F32)
    normed, scale = centre(coarse, row("coarse_gain"))
    packed = dot(normed, vm["coarse_qkv"][...]) * scale
    q = (packed[:, 0:CC] * Q_SCALE).astype(BF)
    k = packed[:, CC : 2 * CC].astype(BF)
    v = packed[:, 2 * CC : 3 * CC].astype(BF)
    heads = []
    for level in range(2):
        at = slice(level * PAD, (level + 1) * PAD)
        parts = []
        for j in range(3):
            cut = slice(j * 128, (j + 1) * 128)
            far = far_v[level, 0, :, 0 : 4 * PAD]
            parts.append(attend4(q[at, cut], k[at, cut], v[at, cut], ones4[...], masks, far).astype(BF))
        heads.append(jnp.concatenate(parts, axis=1))
    heads = jnp.concatenate(heads, axis=0)
    coarse_out = (coarse + dot(heads, vm["coarse_proj"][...])).astype(BF)
    lifted = [dot(coarse_out, up_pad[:, k * 256 : k * 256 + C]) for k in range(4)]
    normed = [centre(x, row("up_gain")) for x in lifted]
    branch = dot(jnp.concatenate([n for n, _ in normed], axis=0), vm["out_weight"][...])
    encoded = [(group[k] + branch[k * 2 * PAD : (k + 1) * 2 * PAD] * normed[k][1]).astype(BF) for k in range(4)]
    three, mines = [], []
    for level in range(2):
        mine = [encoded[k ^ MIRROR[level]][level * PAD : (level + 1) * PAD] for k in range(4)]
        mine = jnp.concatenate(mine, axis=0)
        snd3[level] = dot(vm["send3"][PAD : 4 * PAD], mine).astype(BF)
        three.append(send(2, level, (0, 1, 2), snd3, buf3, ENCODED))
        mines.append(mine)
    mines = [dot(vm["send3"][0:PAD], mine).astype(BF) for mine in mines]
    mines = [dot(vm["final"][level], mines[level]) for level in range(2)]
    for level in range(2):
        for copy in three[level].values():
            copy.wait_recv()
        out_ref[level] = (mines[level] + dot(vm["final_b"][level], buf3[level])).astype(BF)
    for copies in one + two + three:
        for copy in copies.values():
            copy.wait_send()


def body(lat_n, lon_n, tokens, norm_gain, qkv_weight, proj_weight, merge_gain, merge_weight, coarse_gain, *rest):
    coarse_qkv, coarse_proj, up_weight, up_gain, out_weight = rest
    table = tables()
    args = [
        tokens.reshape(2, OWN, C),
        norm_gain,
        qkv_weight,
        proj_weight,
        merge_gain,
        merge_weight,
        coarse_gain,
        coarse_qkv,
        coarse_proj,
        up_weight,
        up_gain,
        out_weight,
    ] + [jnp.asarray(table[n]) for n in TABLES]
    scratch = [pltpu.VMEM(a.shape, a.dtype) for a in args[1:]]
    scratch += [
        pltpu.VMEM((C, 768), BF),
        pltpu.VMEM((CC, 1024), BF),
        pltpu.VMEM((2, 2, PAD, 6 * PAD), F32),
        pltpu.VMEM((2, OWN + HALO, C), BF),
        pltpu.VMEM((2, 4 * PAD + HALO2, C), BF),
        pltpu.VMEM((2, 3 * PAD, C), BF),
        pltpu.VMEM((2, HALO, C), BF),
        pltpu.VMEM((2, 3 * PAD, C), BF),
        pltpu.SemaphoreType.DMA((len(args) - 1,)),
        pltpu.SemaphoreType.DMA((2,)),
        pltpu.SemaphoreType.DMA((3, 2, 5)),
        pltpu.SemaphoreType.DMA((3, 2, 5)),
    ]
    out = pl.pallas_call(
        functools.partial(kernel, lat_n, lon_n),
        out_shape=jax.ShapeDtypeStruct((2, OWN, C), BF),
        in_specs=[pl.BlockSpec(memory_space=pltpu.HBM)] * len(args),
        out_specs=pl.BlockSpec(memory_space=pltpu.VMEM),
        scratch_shapes=scratch,
        compiler_params=pltpu.CompilerParams(
            collective_id=0, has_side_effects=True, vmem_limit_bytes=40 * 1024 * 1024
        ),
    )(*[pltpu.with_memory_space_constraint(a, pltpu.HBM) for a in args])
    return out.reshape(tokens.shape)


def solution(mesh):
    placed = (P(None, "lat", "lon", None),) + (P(),) * 11
    return jax.shard_map(
        functools.partial(body, mesh.shape["lat"], mesh.shape["lon"]),
        mesh=mesh,
        in_specs=placed,
        out_specs=P(None, "lat", "lon", None),
        check_vma=False,
    )
```

```python
import functools

import jax
import jax.numpy as jnp
import ml_dtypes
import numpy as np
from jax import lax
from jax.experimental import pallas as pl
from jax.experimental.pallas import tpu as pltpu
from jax.sharding import PartitionSpec as P

MESH = pl.DeviceIdType.MESH
BF = jnp.bfloat16
F32 = jnp.float32
EPSILON = 1e-05
C = 192
CC = 384
ROWS, COLS = 12, 24
OWN = ROWS * COLS
UNIT = 18
WIN = 72
PAD = 80
HEAD = 32
Q_SCALE = float(HEAD**-0.5 * np.log2(np.e))
V_SCALE = 2.0**-8
FAR = -1e30
HALO = 176
LAT_AT, LON_AT, LON_LAST, DIAG_AT = 0, 64, 112, 144
HALO2 = 192
MIRROR = (2, 3)
SOON = 4 * PAD + 144
RESULTS = (
    (0, 4 * PAD, 32, 2),
    (16, 4 * PAD + 32, 32, 0),
    (32, 4 * PAD + 64, 32, 1),
    (PAD, 4 * PAD + 144, 48, 0),
    (2 * PAD, 4 * PAD + 96, 48, 1),
)
TOKENS = (
    (LON_AT, OWN + LON_AT, 48, 1),
    (LAT_AT, OWN + LAT_AT, 64, 0),
    (DIAG_AT, OWN + DIAG_AT, 32, 2),
    (LON_LAST, OWN + LON_LAST, 32, 1),
)
ENCODED = ((PAD, PAD, PAD, 0), (2 * PAD, 2 * PAD, PAD, 2), (0, 0, PAD, 1))


def one_hot(rows, cols, pairs):
    out = np.zeros((rows, cols), np.float32)
    for r, c in pairs:
        out[r, c] = 1.0
    return out.astype(ml_dtypes.bfloat16)


def halo_slot():
    for j in range(3):
        yield LAT_AT + j * UNIT, (0, j + 1)
        yield (LON_LAST if j == 2 else LON_AT + j * UNIT), (j + 1, 0)
    yield DIAG_AT, (0, 0)


def received(a, b):
    if a == 3 and b == 3:
        return DIAG_AT
    if a == 3:
        return LAT_AT + b * UNIT
    if b == 3:
        return LON_LAST if a == 2 else LON_AT + a * UNIT
    return None


def window_row(a, b):
    window, inner = (a // 2) * 2 + b // 2, (a % 2) * 2 + b % 2
    if window == 2:
        inner = (b % 2) * 2 + a % 2
    return window * PAD + inner * UNIT


def arrival(a, b):
    if a < 3 and b < 3:
        return window_row(a + 1, b + 1)
    which = {(3, 0): 1, (3, 1): 3, (3, 2): 3, (0, 3): 2, (1, 3): 4, (2, 3): 4, (3, 3): 0}[a, b]
    theirs = window_row(0 if a == 3 else a + 1, 0 if b == 3 else b + 1)
    return RESULTS[which][1] + theirs - RESULTS[which][0]


def natural(level, r, c):
    return (r if level == 0 else ROWS - 1 - r) * COLS + COLS - 1 - c


@functools.cache
def tables():
    units = [(a, b) for a in range(4) for b in range(4)]
    send1, gather1, final = [], [], []
    for level in range(2):

        def own(a, b, t, level=level):
            return natural(level, a * 3 + t // 6, b * 6 + t % 6)

        send1.append(
            one_hot(HALO, OWN, [(s + t, own(a, b, t)) for s, (a, b) in halo_slot() for t in range(UNIT)])
        )
        pairs = []
        for a, b in units:
            slot = received(a, b)
            for t in range(UNIT):
                source = own(a + 1, b + 1, t) if slot is None else OWN + slot + t
                pairs.append((window_row(a, b) + t, source))
        gather1.append(one_hot(4 * PAD, OWN + HALO, pairs))
        pairs = []
        for r in range(ROWS):
            for c in range(COLS):
                qr, qc = int(r < 6), int(c < 12)
                y, x = r % 6, c % 12
                k = y % 2 + 2 * (x % 2)
                t = (y // 2) * 6 + x // 2
                pairs.append((natural(level, r, c), (qr * 2 + qc) * PAD + k * UNIT + t))
        final.append(one_hot(OWN, 4 * PAD, pairs))
    pairs = []
    for y in range(ROWS):
        for x in range(COLS):
            a, b, t = y // 3, x // 6, (y % 3) * 6 + x % 6
            source = arrival(a, b) + t
            k = y % 2 + 2 * (x % 2)
            i, j = y // 2, x // 2
            cell = ((i // 3) * 2 + j // 6) * UNIT + (i % 3) * 6 + j % 6
            pairs.append((k * PAD + cell, source))
    gather2 = one_hot(4 * PAD, 4 * PAD + HALO2, pairs)
    pairs = []
    for quarter in range(4):
        for k in range(4):
            for t in range(UNIT):
                pairs.append((quarter * PAD + k * UNIT + t, k * PAD + quarter * UNIT + t))
    send3 = one_hot(4 * PAD, 4 * PAD, pairs)
    ones4 = np.zeros((4 * PAD, 128), np.float32)
    ones2 = np.zeros((224, 128), np.float32)
    for h in range(4):
        ones4[h * PAD : h * PAD + WIN, h * HEAD : (h + 1) * HEAD] = 1.0
    for h in range(2):
        ones2[64 + h * PAD : 64 + h * PAD + WIN, h * HEAD : (h + 1) * HEAD] = 1.0
    ones2[64 : 64 + WIN, 2 * HEAD :] = 1.0
    far = []
    for by_column in (False, True):
        units_of = np.arange(PAD) // UNIT
        side = (units_of % 2 if by_column else units_of // 2) == 1
        far.append(np.where(side[:, None] != np.tile(side, 6)[None, :], np.float32(FAR), np.float32(0.0)))
    far = np.stack(far)
    return dict(
        send1=np.stack(send1),
        gather1=np.stack(gather1),
        gather2=gather2[:, 0:SOON],
        gather2b=gather2[:, SOON:],
        lon1=np.stack(gather1)[:, PAD : 2 * PAD, OWN + LON_AT : OWN + LON_LAST],
        send3=send3,
        final=np.stack(final)[:, :, 0:PAD],
        final_b=np.stack(final)[:, :, PAD:],
        ones4=ones4.astype(ml_dtypes.bfloat16),
        ones2=ones2.astype(ml_dtypes.bfloat16),
        far=far.astype(ml_dtypes.bfloat16),
    )


ARGUMENTS = ("tokens", "norm_gain", "qkv_weight", "proj_weight", "merge_gain", "merge_weight", "coarse_gain", "coarse_qkv")
ARGUMENTS += ("coarse_proj", "up_weight", "up_gain", "out_weight")
EARLY = ("send1", "norm_gain", "qkv_weight", "far", "ones4", "ones2", "proj_weight", "gather1", "lon1")
TABLES = ("send1", "gather1", "gather2", "gather2b", "lon1", "send3", "final", "final_b", "ones4", "ones2", "far")


def dot(a, b):
    return jnp.dot(a, b, preferred_element_type=F32)


def centre(values, gain):
    centred = values - jnp.mean(values, axis=-1, keepdims=True)
    spread = jnp.mean(centred * centred, axis=-1, keepdims=True)
    return (centred * gain).astype(BF), lax.rsqrt(spread + EPSILON)


def dot_t(a, b):
    return lax.dot_general(a, b, (((1,), (1,)), ((), ())), preferred_element_type=F32)


def shared(raised, values, ones):
    both = dot(raised, jnp.concatenate([values, ones], axis=1))
    return both[:, 0:128] / (both[:, 128:256] * V_SCALE)


def attend4(q, k, v, ones4, masks, far):
    keys = jnp.concatenate([k * m for m in masks], axis=0)
    raised = jnp.exp2(dot_t(q, keys) + far).astype(BF)
    small = v * jnp.bfloat16(V_SCALE)
    return shared(raised, jnp.concatenate([small * m for m in masks], axis=0), ones4)


def attend6(q, k, v, ones4, ones2, masks, far):
    zero = jnp.zeros((PAD, 128), BF)
    k0, k1 = k[:, 0:128], k[:, 128:256]
    keys = [jnp.concatenate([k0 * m, zero], axis=1) for m in masks]
    keys += [jnp.concatenate([zero, k1 * m], axis=1) for m in masks[0:2]]
    scores = dot_t(q, jnp.concatenate(keys, axis=0))
    if far is not None:
        scores = scores + far
    raised = jnp.exp2(scores).astype(BF)
    small = v * jnp.bfloat16(V_SCALE)
    v0, v1 = small[:, 0:128], small[:, 128:256]
    first = shared(raised[:, 0 : 4 * PAD], jnp.concatenate([v0 * m for m in masks], axis=0), ones4)
    last = [zero[0:64]] + [v1 * m for m in masks[0:2]]
    last = shared(raised[:, 256 : 6 * PAD], jnp.concatenate(last, axis=0), ones2)
    return jnp.concatenate([first, last], axis=1).astype(BF)


def kernel(lat_n, lon_n, *refs):
    names = list(ARGUMENTS)
    names += list(TABLES)
    hbm = dict(zip(names, refs))
    out_ref = refs[len(names)]
    scratch = refs[len(names) + 1 :]
    vm = dict(zip(names[1:], scratch))
    (qkv_pad, up_pad, far_v, buf1, buf2, buf3, snd1, snd3, load_sem, tok_sem, send_sem, recv_sem) = scratch[
        len(names) - 1 :
    ]

    lat, lon = lax.axis_index("lat"), lax.axis_index("lon")
    up, down = lax.rem(lat + 1, lat_n), lax.rem(lat + lat_n - 1, lat_n)
    east, west = lax.rem(lon + 1, lon_n), lax.rem(lon + lon_n - 1, lon_n)
    takers = (((down, lon), (lat, east), (down, east)), ((up, lon), (lat, east), (up, east)))
    owners = (((up, lon), (lat, west), (up, west)), ((down, lon), (lat, west), (down, west)))

    barrier = pltpu.get_barrier_semaphore()
    for device in ((up, lon), (down, lon), (lat, east), (lat, west)) + tuple((a, b) for a in (up, down) for b in (east, west)):
        pl.semaphore_signal(barrier, inc=1, device_id=device, device_id_type=MESH)

    loads = {}
    for level in range(2):
        loads["tokens", level] = pltpu.make_async_copy(
            hbm["tokens"].at[level], buf1.at[level, pl.ds(0, OWN)], tok_sem.at[level]
        )
        loads["tokens", level].start()
    order = ["send1"] + [n for n in EARLY if n != "send1"]
    order += [n for n in names[1:] if n not in order]

    def load(*wanted):
        for n in wanted:
            loads[n] = pltpu.make_async_copy(hbm[n], vm[n], load_sem.at[order.index(n)])
            loads[n].start()

    load(*order)

    def need(*wanted):
        for n in wanted:
            loads.pop(n).wait()

    def row(n):
        return vm[n][...].reshape(1, -1)

    def send(stage, level, which, source, target, plan):
        devices = (takers if stage < 2 else owners)[level]
        copies = {}
        for i in which:
            start, place, rows, neighbour = plan[i]
            copies[i] = pltpu.make_async_remote_copy(
                src_ref=source.at[level, pl.ds(start, rows)],
                dst_ref=target.at[level, pl.ds(place, rows)],
                send_sem=send_sem.at[stage, level, i],
                recv_sem=recv_sem.at[stage, level, i],
                device_id=devices[neighbour],
                device_id_type=MESH,
            )
            copies[i].start()
        return copies

    need("send1")
    for level in range(2):
        need(("tokens", level))
        snd1[level] = dot(vm["send1"][level], buf1[level, 0:OWN]).astype(BF)
    pl.semaphore_wait(barrier, 8)
    one = [{}, {}]
    for i in (0, 1, 2, 3):
        for level in range(2):
            one[level].update(send(0, level, (i,), snd1, buf1, TOKENS))

    need("qkv_weight", "far")
    zero = jnp.zeros((C, 64), BF)
    for part in range(3):
        qkv_pad[:, part * 256 : part * 256 + C] = vm["qkv_weight"][:, part * C : (part + 1) * C]
        qkv_pad[:, part * 256 + C : (part + 1) * 256] = zero
    edge = (lat_n - 1, 0)
    for level in range(2):
        far_v[level] = jnp.where(lat == edge[level], vm["far"][...].astype(F32), 0.0)
    need("norm_gain", "ones4", "ones2", "proj_weight", "gather1", "lon1")
    lane = lax.broadcasted_iota(jnp.int32, (PAD, 128), 1)
    masks = [jnp.where(lane // HEAD == h, 1.0, 0.0).astype(BF) for h in range(4)]
    ones4, ones2 = vm["ones4"], vm["ones2"]

    def fine(tokens, items):
        normed, scale = centre(tokens, row("norm_gain"))
        packed = dot(normed, qkv_pad[...]) * scale
        q = (packed[:, 0:256] * Q_SCALE).astype(BF)
        k = packed[:, 256:512].astype(BF)
        v = packed[:, 512:768].astype(BF)
        heads = []
        for i, (level, w) in enumerate(items):
            at = slice(i * PAD, (i + 1) * PAD)
            far = far_v[level, 3 - w] if w >= 2 else None
            heads.append(attend6(q[at], k[at], v[at], ones4[...], ones2[...], masks, far))
        heads = jnp.concatenate(heads, axis=0)[:, 0:C]
        result = (tokens + dot(heads, vm["proj_weight"][...])).astype(BF)
        for i, (level, w) in enumerate(items):
            buf2[level, w * PAD : (w + 1) * PAD] = result[i * PAD : (i + 1) * PAD]

    first = [dot(vm["gather1"][level, 0:PAD, 0:OWN], buf1[level, 0:OWN]) for level in range(2)]
    fine(jnp.concatenate(first, axis=0), [(0, 0), (1, 0)])

    two = [send(1, level, (0, 1, 2), buf2, buf2, RESULTS) for level in range(2)]

    own = [dot(vm["gather1"][level, PAD : 2 * PAD, 0:OWN], buf1[level, 0:OWN]) for level in range(2)]
    for level in range(2):
        one[level][0].wait_recv()
    near, nearer = OWN + LON_AT, OWN + LON_LAST
    rest = [own[level] + dot(vm["lon1"][level], buf1[level, near:nearer]) for level in range(2)]
    fine(jnp.concatenate(rest, axis=0), [(0, 1), (1, 1)])
    for level in range(2):
        two[level].update(send(1, level, (3,), buf2, buf2, RESULTS))
    near = OWN + LON_AT
    for level in range(2):
        one[level][1].wait_recv()
    rest = [dot(vm["gather1"][level, 2 * PAD : 3 * PAD, 0:near], buf1[level, 0:near]) for level in range(2)]
    fine(jnp.concatenate(rest, axis=0), [(0, 2), (1, 2)])
    for level in range(2):
        two[level].update(send(1, level, (4,), buf2, buf2, RESULTS))
    for level in range(2):
        one[level][3].wait_recv()
        one[level][2].wait_recv()
    last = [dot(vm["gather1"][level, 3 * PAD : 4 * PAD], buf1[level]) for level in range(2)]
    fine(jnp.concatenate(last, axis=0), [(0, 3), (1, 3)])

    need("up_weight")
    for k in range(4):
        up_pad[:, k * 256 : k * 256 + C] = vm["up_weight"][:, k * C : (k + 1) * C]
    need("gather2", "send3", "merge_gain", "merge_weight", "coarse_gain", "coarse_qkv", "coarse_proj")
    need("up_gain", "out_weight", "final", "final_b", "gather2b")

    for level in range(2):
        for i in (0, 1, 2, 4):
            two[level][i].wait_recv()
    soon = [dot(vm["gather2"][...], buf2[level, 0:SOON]) for level in range(2)]
    for level in range(2):
        two[level][3].wait_recv()
    cells = [soon[level] + dot(vm["gather2b"][...], buf2[level, SOON:]) for level in range(2)]
    group = [
        jnp.concatenate([cells[level][(k ^ m) * PAD : ((k ^ m) + 1) * PAD] for level, m in enumerate(MIRROR)], axis=0)
        for k in range(4)
    ]
    average = jnp.sum(group[0] + group[1] + group[2] + group[3], axis=-1, keepdims=True) * (1.0 / (4 * C))
    centred = [g - average for g in group]
    squares = [c * c for c in centred]
    spread = jnp.sum(squares[0] + squares[1] + squares[2] + squares[3], axis=-1, keepdims=True) * (1.0 / (4 * C))
    scale = lax.rsqrt(spread + EPSILON)
    coarse = jnp.zeros((2 * PAD, CC), F32)
    for k in range(4):
        stacked = (centred[k] * row("merge_gain")[:, k * C : (k + 1) * C]).astype(BF)
        coarse = coarse + dot(stacked, vm["merge_weight"][k * C : (k + 1) * C])
    coarse = (coarse * scale).astype(BF).astype(F32)
    normed, scale = centre(coarse, row("coarse_gain"))
    packed = dot(normed, vm["coarse_qkv"][...]) * scale
    q = (packed[:, 0:CC] * Q_SCALE).astype(BF)
    k = packed[:, CC : 2 * CC].astype(BF)
    v = packed[:, 2 * CC : 3 * CC].astype(BF)
    heads = []
    for level in range(2):
        at = slice(level * PAD, (level + 1) * PAD)
        parts = []
        for j in range(3):
            cut = slice(j * 128, (j + 1) * 128)
            far = far_v[level, 0, :, 0 : 4 * PAD]
            parts.append(attend4(q[at, cut], k[at, cut], v[at, cut], ones4[...], masks, far).astype(BF))
        heads.append(jnp.concatenate(parts, axis=1))
    heads = jnp.concatenate(heads, axis=0)
    coarse_out = (coarse + dot(heads, vm["coarse_proj"][...])).astype(BF)
    lifted = [dot(coarse_out, up_pad[:, k * 256 : k * 256 + C]) for k in range(4)]
    normed = [centre(x, row("up_gain")) for x in lifted]
    branch = dot(jnp.concatenate([n for n, _ in normed], axis=0), vm["out_weight"][...])
    encoded = [(group[k] + branch[k * 2 * PAD : (k + 1) * 2 * PAD] * normed[k][1]).astype(BF) for k in range(4)]
    three, mines = [], []
    for level in range(2):
        mine = [encoded[k ^ MIRROR[level]][level * PAD : (level + 1) * PAD] for k in range(4)]
        mine = jnp.concatenate(mine, axis=0)
        snd3[level] = dot(vm["send3"][PAD : 4 * PAD], mine).astype(BF)
        three.append(send(2, level, (0, 1, 2), snd3, buf3, ENCODED))
        mines.append(mine)
    mines = [dot(vm["send3"][0:PAD], mine).astype(BF) for mine in mines]
    mines = [dot(vm["final"][level], mines[level]) for level in range(2)]
    for level in range(2):
        for copy in three[level].values():
            copy.wait_recv()
        out_ref[level] = (mines[level] + dot(vm["final_b"][level], buf3[level])).astype(BF)
    for copies in one + two + three:
        for copy in copies.values():
            copy.wait_send()


def body(lat_n, lon_n, tokens, norm_gain, qkv_weight, proj_weight, merge_gain, merge_weight, coarse_gain, *rest):
    coarse_qkv, coarse_proj, up_weight, up_gain, out_weight = rest
    table = tables()
    args = [
        tokens.reshape(2, OWN, C),
        norm_gain,
        qkv_weight,
        proj_weight,
        merge_gain,
        merge_weight,
        coarse_gain,
        coarse_qkv,
        coarse_proj,
        up_weight,
        up_gain,
        out_weight,
    ] + [jnp.asarray(table[n]) for n in TABLES]
    scratch = [pltpu.VMEM(a.shape, a.dtype) for a in args[1:]]
    scratch += [
        pltpu.VMEM((C, 768), BF),
        pltpu.VMEM((CC, 1024), BF),
        pltpu.VMEM((2, 2, PAD, 6 * PAD), F32),
        pltpu.VMEM((2, OWN + HALO, C), BF),
        pltpu.VMEM((2, 4 * PAD + HALO2, C), BF),
        pltpu.VMEM((2, 3 * PAD, C), BF),
        pltpu.VMEM((2, HALO, C), BF),
        pltpu.VMEM((2, 3 * PAD, C), BF),
        pltpu.SemaphoreType.DMA((len(args) - 1,)),
        pltpu.SemaphoreType.DMA((2,)),
        pltpu.SemaphoreType.DMA((3, 2, 5)),
        pltpu.SemaphoreType.DMA((3, 2, 5)),
    ]
    out = pl.pallas_call(
        functools.partial(kernel, lat_n, lon_n),
        out_shape=jax.ShapeDtypeStruct((2, OWN, C), BF),
        in_specs=[pl.BlockSpec(memory_space=pltpu.HBM)] * len(args),
        out_specs=pl.BlockSpec(memory_space=pltpu.VMEM),
        scratch_shapes=scratch,
        compiler_params=pltpu.CompilerParams(
            collective_id=0, has_side_effects=True, vmem_limit_bytes=40 * 1024 * 1024
        ),
    )(*[pltpu.with_memory_space_constraint(a, pltpu.HBM) for a in args])
    return out.reshape(tokens.shape)


def solution(mesh):
    placed = (P(None, "lat", "lon", None),) + (P(),) * 11
    return jax.shard_map(
        functools.partial(body, mesh.shape["lat"], mesh.shape["lon"]),
        mesh=mesh,
        in_specs=placed,
        out_specs=P(None, "lat", "lon", None),
        check_vma=False,
    )
```
